256 devices in a mesh: group: 8 (over y, core), tensor: 32 (over z, x).
Axes of the slice: x: 4, y: 4, z: 8, core: 2. Of those that a mesh axis runs over, the one named last changes fastest.
Arguments:
- inputs: bfloat16 [3, 2048, 8192], P(None, ('group', 'tensor')), may hold values from -500 to 500
- norm_gain: bfloat16 [8192], replicated, may hold values from 0.099609375 to 1.8984375
- united_weight: bfloat16 [8192, 10240], P(None, 'tensor'), may hold values from -0.0625 to 0.0625
- adapter_down: bfloat16 [192, 8192, 128], P('group', 'tensor'), may hold values from -0.0625 to 0.0625
- query_up: bfloat16 [192, 64, 8192], P('group', None, 'tensor'), may hold values from -0.75 to 0.75
- value_up: bfloat16 [192, 64, 1024], P('group', None, 'tensor'), may hold values from -0.75 to 0.75
- history: bfloat16 [2048, 256, 2048], P(('group', 'tensor')), may hold values from -256 to 256
- adapter_slot: int32 [192], replicated, may hold values from 0 to 191, as said below
- row_adapter: int32 [2048], P('group'), may hold values from 0 to 191, as said below
- cache_length: int32 [2048], P('group'), may hold values from 2 to 256, as said below
Outputs:
- context: bfloat16 [3, 2048, 8192], P(None, ('group', 'tensor'))
The draws below stay inside these ranges and needn't reach their ends.
Inputs may be any that keep to these rules, and one draw needn't show every extreme that they name: `adapter_slot`: each adapter has its own slot; slot s lies in group s // 24. `row_adapter`: row r belongs to group r // 256; all rows of one adapter lie in one group. For each ordered pair of groups, the rows of the first use at most 2 distinct adapters whose slots lie in the second, and some pair reaches 2. `cache_length`: some row reaches 256.
All inputs are finite; a program needn't handle non-finite values.
Results may differ from the reference program's by a relative error of at most 0.012.
The reference program's roundings to bfloat16 on the way count: a program that leaves them out, or rounds other values in their place, can miss the bound.
Values may be sent and summed in bfloat16 or wider, within the bound.
A program may use at most 192 MiB of HBM per device.

```python
import math
import jax
import jax.numpy as jnp
from jax import lax

D = 8192
HEADS = 64
KV_HEADS = 8
HEAD_DIM = 128
RANK = 64
STEPS = 3
PAIR_MOST = 2
CACHE = 256
ADAPT_GRP = 24
ROWS_GRP = 256
ROWS = 2048
ADAPTERS = 192
KVD = 1024
QKV = 10240
N_GROUP = 8
N_TENSOR = 32


def layout(key):
    streams = jax.random.split(key, 9)
    group_ids = jnp.arange(N_GROUP, dtype=jnp.int32)
    adapter_slot = jax.random.permutation(streams[0], ADAPTERS).astype(jnp.int32)
    slot_adapter = jnp.zeros((ADAPTERS,), jnp.int32).at[adapter_slot].set(jnp.arange(ADAPTERS, dtype=jnp.int32))
    counts = jax.random.randint(streams[1], (N_GROUP, N_GROUP), 0, PAIR_MOST + 1)
    hot_source = jax.random.randint(streams[2], (), 0, N_GROUP)
    hot_target = (hot_source + jax.random.randint(streams[3], (), 1, N_GROUP)) % N_GROUP
    counts = counts.at[hot_source, hot_target].set(PAIR_MOST)
    counts = jnp.where(group_ids[:, None] == group_ids[None, :], 0, counts)
    local_order = jax.vmap(lambda subkey: jax.random.permutation(subkey, ADAPT_GRP))(jax.random.split(streams[4], N_GROUP)).astype(jnp.int32)
    lanes = jnp.arange(N_GROUP * PAIR_MOST, dtype=jnp.int32)
    lane_target = lanes // PAIR_MOST
    lane_rank = lanes % PAIR_MOST
    moving = lane_rank[None, :] < counts[:, lane_target]
    mover_place = local_order[:, :N_GROUP * PAIR_MOST]
    slot_target = jnp.broadcast_to(group_ids[:, None], (N_GROUP, ADAPT_GRP))
    slot_target = slot_target.at[group_ids[:, None], mover_place].set(jnp.where(moving, lane_target[None, :], group_ids[:, None]))
    staying = slot_target == group_ids[:, None]
    shuffle = jax.vmap(lambda subkey: jax.random.permutation(subkey, ADAPT_GRP))(jax.random.split(streams[5], N_GROUP)).astype(jnp.int32)
    ordering = jnp.argsort(jnp.where(staying, 0, ADAPT_GRP) + shuffle, axis=1).astype(jnp.int32)
    stay_count = jnp.sum(staying.astype(jnp.int32), axis=1)
    pick_one = jax.random.randint(streams[6], (N_GROUP, ROWS_GRP), 0, stay_count[:, None])
    pick_two = jax.random.randint(streams[7], (N_GROUP, ROWS_GRP), 0, stay_count[:, None])
    picks = jnp.minimum(pick_one, pick_two)
    stay_slot = group_ids[:, None] * ADAPT_GRP + jnp.take_along_axis(ordering, picks, axis=1)
    arriving = mover_place.reshape(N_GROUP, N_GROUP, PAIR_MOST).transpose(1, 0, 2)
    arriving_slot = (group_ids[None, :, None] * ADAPT_GRP + arriving).reshape(N_GROUP, N_GROUP * PAIR_MOST)
    arriving_live = (jnp.arange(PAIR_MOST, dtype=jnp.int32)[None, None, :] < counts.T[:, :, None]).reshape(N_GROUP, N_GROUP * PAIR_MOST)
    head_rows = jnp.where(arriving_live, arriving_slot, stay_slot[:, :N_GROUP * PAIR_MOST])
    row_slot = jnp.concatenate([head_rows, stay_slot[:, N_GROUP * PAIR_MOST:]], axis=1)
    row_order = jax.vmap(lambda subkey: jax.random.permutation(subkey, ROWS_GRP))(jax.random.split(streams[8], N_GROUP)).astype(jnp.int32)
    row_slot = jnp.take_along_axis(row_slot, row_order, axis=1)
    return (adapter_slot, slot_adapter[row_slot].reshape(ROWS).astype(jnp.int32))


def draw_adapter_slot(key, part):
    shared = layout(key)
    return shared[0]


def draw_row_adapter(key, part):
    shared = layout(key)
    return shared[1]


def draw_cache_length(key, part):
    key = jax.random.fold_in(key, 37)
    streams = jax.random.split(key, 2)
    lengths = jax.random.randint(streams[0], (ROWS,), 2, CACHE + 1)
    longest = jax.random.randint(streams[1], (), 0, ROWS)
    return lengths.at[longest].set(CACHE).astype(jnp.int32)


def draw_inputs(key, part):
    key = jax.random.fold_in(key, 11)
    streams = jax.random.split(key, 3)
    entries = jnp.clip(jax.random.normal(streams[0], (STEPS, ROWS, D), jnp.float32), -4.0, 4.0)
    row_scale = jnp.exp(jax.random.uniform(streams[1], (STEPS, ROWS, 1), jnp.float32, 0.0, math.log(10.0)))
    column_scale = jnp.exp(jax.random.uniform(streams[2], (D,), jnp.float32, 0.0, math.log(10.0)))
    values = row_scale * column_scale * entries
    return values.astype(jnp.bfloat16)


def draw_history(key, part):
    key = jax.random.fold_in(key, 23)
    streams = jax.random.split(key, 1)
    kv_width = KV_HEADS * HEAD_DIM
    values = jnp.clip(jax.random.normal(streams[0], (ROWS, CACHE, 2 * kv_width), jnp.float32), -4.0, 4.0)
    return values.astype(jnp.bfloat16)


def shard_levels(own_key, extent, cuts, smallest, top_value):
    def one(position, parts):
        heights = jax.random.uniform(jax.random.fold_in(jax.random.fold_in(own_key, 6), position), (parts,), jnp.float32, smallest / len(cuts), top_value / len(cuts))
        return jnp.repeat(jnp.exp(heights), extent[position] // parts).reshape((-1,) + (1,) * (len(extent) - position - 1))

    level = one(*cuts[0])
    for cut in cuts[1:]:
        level = level * one(*cut)
    return level


def centred(rng, dims, width, reach, pieces=(), kind=jnp.bfloat16):
    gain = shard_levels(rng, dims, pieces, -0.22, 0.18) if pieces else 1.0
    drawn = jax.random.normal(rng, dims, jnp.float32) * width * gain
    return jnp.minimum(jnp.maximum(drawn, -reach), reach).astype(kind)


def setup_inputs(seed: int = 0) -> dict:
    keys = jax.random.split(jax.random.key(seed), 11)
    inputs = draw_inputs(jax.random.fold_in(keys[10], 71), 0)
    norm_gain = jnp.clip(1.0 + 0.18 * jax.random.normal(keys[1], (D,), jnp.float32), 0.099609375, 1.8984375).astype(jnp.bfloat16)
    united_weight = centred(keys[2], (D, QKV), D ** -0.5, 0.0625, ((1, 32),))
    adapter_down = centred(keys[3], (ADAPTERS, D, 2 * RANK), D ** -0.5, 0.0625, ((0, 8), (1, 32)))
    query_up = centred(keys[4], (ADAPTERS, RANK, D), RANK ** -0.5, 0.75, ((0, 8), (2, 32)))
    value_up = centred(keys[5], (ADAPTERS, RANK, KVD), RANK ** -0.5, 0.75, ((0, 8), (2, 32)))
    history = draw_history(jax.random.fold_in(keys[10], 71), 0)
    adapter_slot = draw_adapter_slot(jax.random.fold_in(keys[10], 71), 0)
    row_adapter = draw_row_adapter(jax.random.fold_in(keys[10], 71), 0)
    cache_length = draw_cache_length(jax.random.fold_in(keys[10], 71), 0)
    return dict(inputs=inputs, norm_gain=norm_gain, united_weight=united_weight, adapter_down=adapter_down, query_up=query_up, value_up=value_up, history=history, adapter_slot=adapter_slot, row_adapter=row_adapter, cache_length=cache_length)


adapter_scale = 0.5
rope_base = 500000.0
norm_eps = 1e-05

def batched_product(pattern, first_operand, second_operand):
    return jnp.einsum(pattern, lax.optimization_barrier(first_operand).astype(jnp.float32), lax.optimization_barrier(second_operand).astype(jnp.float32))

def rms_normed(inputs, norm_gain):
    values = inputs.astype(jnp.float32)
    mean_square = lax.optimization_barrier(jnp.mean(values * values, axis=-1, keepdims=True))
    return (values * lax.rsqrt(mean_square + norm_eps) * norm_gain.astype(jnp.float32)).astype(jnp.bfloat16)

def rotate(heads_in, positions):
    head_width = heads_in.shape[-1]
    halfway = head_width // 2
    ladder = jnp.arange(halfway).astype(jnp.float32) * (2.0 / head_width)
    inverse = jnp.power(jnp.float32(rope_base), -ladder)
    angles = positions.astype(jnp.float32)[..., None, None] * inverse
    cosine = jnp.cos(angles)
    sine_part = jnp.sin(angles)
    values = heads_in.astype(jnp.float32)
    leading = values[..., :halfway]
    trailing = values[..., halfway:]
    turned = jnp.concatenate([leading * cosine - trailing * sine_part, trailing * cosine + leading * sine_part], axis=-1)
    return turned.astype(jnp.bfloat16)

def attend(queries, new_keys, new_values, history, lengths, current):
    row_count, head_count, head_width = queries.shape
    kv_count = new_keys.shape[2]
    kv_width = kv_count * head_width
    window = history.shape[1]
    past_keys = history[:, :, :kv_width].reshape(row_count, window, kv_count, head_width)
    past_values = history[:, :, kv_width:].reshape(row_count, window, kv_count, head_width)
    grouped = queries.reshape(row_count, kv_count, head_count // kv_count, head_width)
    factor = head_width ** (-0.5)
    past_scores = batched_product('rkgd,rpkd->rkgp', grouped, past_keys) * factor
    fresh_scores = batched_product('rkgd,jrkd->rkgj', grouped, new_keys) * factor
    past_live = jnp.arange(window)[None, :] < lengths[:, None]
    fresh_live = jnp.arange(new_keys.shape[0]) <= current
    past_scores = jnp.where(past_live[:, None, None, :], past_scores, -jnp.inf)
    fresh_scores = jnp.where(fresh_live, fresh_scores, -jnp.inf)
    highest = jnp.maximum(lax.optimization_barrier(jnp.max(past_scores, axis=-1)), lax.optimization_barrier(jnp.max(fresh_scores, axis=-1)))[..., None]
    past_exp = jnp.exp(past_scores - highest)
    fresh_exp = jnp.exp(fresh_scores - highest)
    denominator = lax.optimization_barrier(jnp.sum(past_exp, axis=-1, keepdims=True)) + lax.optimization_barrier(jnp.sum(fresh_exp, axis=-1, keepdims=True))
    past_weights = (past_exp / denominator).astype(jnp.bfloat16)
    fresh_weights = (fresh_exp / denominator).astype(jnp.bfloat16)
    context = batched_product('rkgp,rpkd->rkgd', past_weights, past_values) + batched_product('rkgj,jrkd->rkgd', fresh_weights, new_values)
    return context.reshape(row_count, head_count * head_width).astype(jnp.bfloat16)

def reference(inputs, norm_gain, united_weight, adapter_down, query_up, value_up, history, adapter_slot, row_adapter, cache_length):
    sections, overall_row_count, model_width = inputs.shape
    shards = N_TENSOR
    kv_width = KV_HEADS * HEAD_DIM
    block_span_width = united_weight.shape[1] // shards
    query_portion = model_width // shards
    key_portion = kv_width // shards
    normed = rms_normed(inputs, norm_gain)
    arranged = united_weight.reshape(model_width, shards, block_span_width)
    query_weight = arranged[:, :, :query_portion].reshape(model_width, model_width)
    key_weight = arranged[:, :, query_portion:query_portion + key_portion].reshape(model_width, kv_width)
    value_weight = arranged[:, :, query_portion + key_portion:].reshape(model_width, kv_width)
    flattened = normed.reshape(sections * overall_row_count, model_width)
    plain_query_rows = jnp.dot(flattened, query_weight, preferred_element_type=jnp.float32).reshape(sections, overall_row_count, model_width)
    base_key = jnp.dot(flattened, key_weight, preferred_element_type=jnp.float32).reshape(sections, overall_row_count, kv_width)
    plain_value_rows = jnp.dot(flattened, value_weight, preferred_element_type=jnp.float32).reshape(sections, overall_row_count, kv_width)
    slot_of_row = adapter_slot[row_adapter].astype(jnp.int32)
    rank_size = query_up.shape[1]
    row_block_span = 16

    def adapter_block_rows(element_total):
        first_row = element_total * row_block_span
        picked = lax.dynamic_slice_in_dim(slot_of_row, first_row, row_block_span, 0)
        block_inputs = lax.dynamic_slice_in_dim(normed, first_row, row_block_span, 1)
        lowrank = batched_product('srd,rdk->srk', block_inputs, adapter_down[picked]).astype(jnp.bfloat16)
        query_adapter_delta = batched_product('srk,rkc->src', lowrank[..., :rank_size], query_up[picked])
        value_adapter_delta = batched_product('srk,rkc->src', lowrank[..., rank_size:], value_up[picked])
        return (query_adapter_delta, value_adapter_delta)
    query_adapter_delta, value_adapter_delta = lax.map(adapter_block_rows, jnp.arange(overall_row_count // row_block_span, dtype=jnp.int32))
    query_adapter_delta = query_adapter_delta.transpose(1, 0, 2, 3).reshape(sections, overall_row_count, model_width)
    value_adapter_delta = value_adapter_delta.transpose(1, 0, 2, 3).reshape(sections, overall_row_count, kv_width)
    query_vectors = (plain_query_rows + adapter_scale * query_adapter_delta).astype(jnp.bfloat16)
    key = base_key.astype(jnp.bfloat16)
    value_vectors = (plain_value_rows + adapter_scale * value_adapter_delta).astype(jnp.bfloat16)
    query_vectors, key = lax.optimization_barrier((query_vectors, key))
    positions = cache_length[None, :] + jnp.arange(sections, dtype=jnp.int32)[:, None]
    rot_query = rotate(query_vectors.reshape(sections, overall_row_count, HEADS, HEAD_DIM), positions)
    rot_key = rotate(key.reshape(sections, overall_row_count, KV_HEADS, HEAD_DIM), positions)
    value_heads = value_vectors.reshape(sections, overall_row_count, KV_HEADS, HEAD_DIM)
    attend_block = 32

    def attention_block(element_total):
        first_row = element_total * attend_block
        block_query = lax.dynamic_slice_in_dim(rot_query, first_row, attend_block, 1)
        block_keys = lax.dynamic_slice_in_dim(rot_key, first_row, attend_block, 1)
        block_values = lax.dynamic_slice_in_dim(value_heads, first_row, attend_block, 1)
        block_history = lax.dynamic_slice_in_dim(history, first_row, attend_block, 0)
        block_lengths = lax.dynamic_slice_in_dim(cache_length, first_row, attend_block, 0)
        return jnp.stack([attend(block_query[step_index], block_keys, block_values, block_history, block_lengths, step_index) for step_index in range(sections)])
    outputs = lax.map(attention_block, jnp.arange(overall_row_count // attend_block, dtype=jnp.int32))
    return outputs.transpose(1, 0, 2, 3).reshape(sections, overall_row_count, model_width)
```

```python
import functools

import jax
import jax.numpy as jnp
from jax import lax
from jax.experimental import pallas as pl
from jax.experimental.pallas import tpu as pltpu
from jax.sharding import PartitionSpec as P

HEADS = 64
KV_HEADS = 8
HEAD_DIM = 128
PAIR_MOST = 2
NX = 4

adapter_scale = 0.5
rope_base = 500000.0
norm_eps = 1e-05
MIB = 1024 * 1024
F32 = jnp.float32
BF16 = jnp.bfloat16
MESH = pl.DeviceIdType.MESH


def rms_normed(inputs, norm_gain):
    values = inputs.astype(F32)
    mean_square = jnp.mean(values * values, axis=-1, keepdims=True)
    return (values * lax.rsqrt(mean_square + norm_eps) * norm_gain.astype(F32)).astype(BF16)


def rotate(heads_in, positions):
    head_width = heads_in.shape[-1]
    halfway = head_width // 2
    ladder = jnp.arange(halfway).astype(F32) * (2.0 / head_width)
    inverse = jnp.power(F32(rope_base), -ladder)
    angles = positions.astype(F32)[..., None, None] * inverse
    cosine = jnp.cos(angles)
    sine_part = jnp.sin(angles)
    values = heads_in.astype(F32)
    leading = values[..., :halfway]
    trailing = values[..., halfway:]
    turned = jnp.concatenate(
        [leading * cosine - trailing * sine_part, trailing * cosine + leading * sine_part], axis=-1
    )
    return turned.astype(BF16)


def project_kernel(
    nx, nz, ng, own,
    xk, xl, w, down, qup, vup, req, tr,
    out,
    X, wv, lbuf, xs, down_o, q_o, v_o, down_f, q_f, v_f, sd, sq, sv, rbuf, rs,
    part, pbuf, S, sbuf, lrz, lrall, LRq, LRv, Dq, Dv, acc, ob,
    ssem, gsem, lsem, dsem, fsem, qsem, p1, p2, p3, p4, osem, wsem,
):
    nt = nx * nz
    K2 = X.shape[1]
    NW = w.shape[1]
    rank = 64
    tiles = K2 // 128
    ta = max((tiles * 13) // 32, 2)
    LA = ta * 128
    LB = K2 - LA
    spans = {
        "A": ((0, (ta // 2) * 128), ((ta // 2) * 128, LA - (ta // 2) * 128)),
        "B": ((LA, ((tiles - ta) // 2) * 128), (LA + ((tiles - ta) // 2) * 128, LB - ((tiles - ta) // 2) * 128)),
    }
    whole = {"A": (0, LA), "B": (LA, LB)}
    which = {"A": 0, "B": 1}

    g = lax.axis_index("group")
    t = lax.axis_index("tensor")
    z = t // nx
    x = t % nx

    def dev(dx, dz):
        return lax.rem(z + (dz % nz), nz) * nx + lax.rem(x + (dx % nx), nx)

    pending = []
    counter = [0]

    def remote(src, dst, rsem, group, tensor):
        sem = ssem.at[counter[0]]
        counter[0] += 1
        copy = pltpu.make_async_remote_copy(
            src_ref=src, dst_ref=dst, send_sem=sem, recv_sem=rsem,
            device_id=(group, tensor), device_id_type=MESH,
        )
        copy.start()
        pending.append(copy)

    def arrived(ref, sem):
        pltpu.make_async_copy(ref, ref, sem).wait()

    barrier = pltpu.get_barrier_semaphore()

    def greet(k, carry):
        pl.semaphore_signal(barrier, inc=1, device_id=(g, lax.rem(t + k, nt)), device_id_type=MESH)
        return carry

    lax.fori_loop(1, nt, greet, 0)

    def greet_group(k, carry):
        pl.semaphore_signal(barrier, inc=1, device_id=(lax.rem(g + k, ng), t), device_id_type=MESH)
        return carry

    lax.fori_loop(1, ng, greet_group, 0)

    mine = pl.multiple_of(t * 48, 16)
    loads = [
        pltpu.make_async_copy(xk, X.at[pl.ds(mine, 48), :], wsem.at[0]),
        pltpu.make_async_copy(down, down_o, wsem.at[1]),
        pltpu.make_async_copy(qup, q_o, wsem.at[2]),
        pltpu.make_async_copy(vup, v_o, wsem.at[3]),
        pltpu.make_async_copy(w.at[pl.ds(0, K2), :], wv.at[0], wsem.at[4]),
        pltpu.make_async_copy(w.at[pl.ds(K2, K2), :], wv.at[1], wsem.at[5]),
        pltpu.make_async_copy(xl.at[pl.ds(mine, 48), :], lbuf.at[pl.ds(mine, 48), :], wsem.at[6]),
    ]
    for load in loads:
        load.start()
    loads[0].wait()

    pl.semaphore_wait(barrier, nt - 1 + ng - 1)

    def piece(dx, dz, lo, n):
        rows = pl.multiple_of(dev(dx, dz) * 48, 16)
        return X.at[pl.ds(rows, 48), pl.ds(lo, n)]

    def forward(name, dx, dz, half, axis, step):
        lo, n = whole[name] if half is None else spans[name][half]
        ref = piece(dx, dz, lo, n)
        if axis == "x":
            there = dev(step, 0)
            ndx, ndz = (dx - step) % nx, dz % nz
        else:
            there = dev(0, step)
            ndx, ndz = dx % nx, (dz - step) % nz
        remote(ref, ref, gsem.at[which[name], ndx, ndz, 0 if half is None else half], g, there)

    def expect(name, dx, dz, half):
        lo, n = whole[name] if half is None else spans[name][half]
        arrived(piece(dx, dz, lo, n), gsem.at[which[name], dx % nx, dz % nz, 0 if half is None else half])

    def launch(name, dx, dz, axis):
        size = nx if axis == "x" else nz
        if size // 2 > 1:
            forward(name, dx, dz, None, axis, 1)
            forward(name, dx, dz, None, axis, -1)
        elif size == 2:
            forward(name, dx, dz, 0, axis, 1)
            forward(name, dx, dz, 1, axis, -1)

    def relay(name, dx, dz, axis, k, sign):
        size = nx if axis == "x" else nz
        if k + 1 < size // 2:
            forward(name, dx, dz, None, axis, -sign)
        elif k + 1 == size // 2:
            forward(name, dx, dz, 0 if sign < 0 else 1, axis, -sign)

    def wave(name, axis, k, other):
        size = nx if axis == "x" else nz
        if k < size // 2:
            for sign in (-1, 1):
                dx, dz = (sign * k, other) if axis == "x" else (other, sign * k)
                expect(name, dx, dz, None)
                relay(name, dx, dz, axis, k, sign)
        elif size > 1:
            dx, dz = (k, other) if axis == "x" else (other, k)
            expect(name, dx, dz, 0)
            expect(name, dx, dz, 1)

    for k in range(1, nt):
        peer = lax.rem(t + k, nt)
        remote(
            xl.at[pl.ds(pl.multiple_of(peer * 48, 16), 48), :],
            lbuf.at[pl.ds(mine, 48), :], lsem.at[nt - k], g, peer,
        )
    for k in range(1, ng):
        peer = lax.rem(g + k, ng)
        remote(req.at[peer], rbuf.at[g], qsem.at[ng - k], peer, t)

    launch("A", 0, 0, "x")
    launch("B", 0, 0, "z")
    launch("B", 0, 0, "x")
    launch("A", 0, 0, "z")

    for load in loads[1:4]:
        load.wait()
    down_f[pl.ds(g * 2, 2)] = jnp.zeros((2,) + down_f.shape[1:], BF16)
    q_f[pl.ds(pl.multiple_of(g * 2 * rank, 16), 2 * rank), :] = jnp.zeros((2 * rank, q_f.shape[1]), BF16)
    v_f[pl.ds(pl.multiple_of(g * 2 * rank, 16), 2 * rank), :] = jnp.zeros((2 * rank, v_f.shape[1]), BF16)
    for k in range(1, ng):
        peer = lax.rem(g + k, ng)
        arrived(rbuf.at[peer], qsem.at[k])
        down_copy = pltpu.make_async_copy(rbuf.at[peer], rs.at[k], wsem.at[7])
        down_copy.start()
        down_copy.wait()
        for j in range(PAIR_MOST):
            slot = rs[k, 0, j]
            sd[k, j] = down_o[slot]
            sq[k, j] = q_o[slot]
            sv[k, j] = v_o[slot]
        here = pl.multiple_of(g * 2 * rank, 16)
        remote(sd.at[k], down_f.at[pl.ds(g * 2, 2)], fsem.at[ng - k, 0], peer, t)
        for j in range(PAIR_MOST):
            spot = pl.ds(pl.multiple_of((g * 2 + j) * rank, 16), rank)
            remote(sq.at[k, j], q_f.at[spot, :], fsem.at[ng - k, 1 + j], peer, t)
            remote(sv.at[k, j], v_f.at[spot, :], fsem.at[ng - k, 3 + j], peer, t)

    wave("A", "x", 1, 0)
    if nx == 4:
        launch("A", 1, 0, "z")
        launch("A", -1, 0, "z")
    wave("B", "z", 1, 0)
    for sign in ((-1, 1) if nz > 2 else (1,)):
        if nz > 1:
            launch("B", 0, sign, "x")
    if nx == 4:
        wave("A", "x", 2, 0)
        launch("A", 2, 0, "z")
    elif nx == 2:
        launch("A", 1, 0, "z")

    loads[6].wait()
    for k in range(1, nt):
        arrived(lbuf.at[pl.ds(pl.multiple_of(lax.rem(t + k, nt) * 48, 16), 48), :], lsem.at[k])
    both = lbuf[...].astype(F32).reshape(nt, 2, 24, 128)
    xs[...] = jnp.concatenate([both[:, 0], both[:, 1]], axis=-1).reshape(nt * 24, 256)

    def shrink(table, first):
        def body(e, carry):
            chosen = tr[...] == e + first
            pick = jnp.concatenate([chosen, chosen], axis=-1)
            rows = jnp.where(pick, xs[...], 0.0).astype(BF16)
            part[...] += jnp.dot(rows, table[e], preferred_element_type=F32)
            return carry
        return body

    part[...] = jnp.zeros(part.shape, F32)
    lax.fori_loop(0, own, shrink(down_o, 0), 0)

    for k in range(2, nz // 2 + 1):
        wave("B", "z", k, 0)
        for sign in ((-1, 1) if k < nz // 2 else (1,)):
            launch("B", 0, sign * k, "x")

    for k in range(1, ng):
        peer = lax.rem(g + k, ng)
        arrived(down_f.at[pl.ds(peer * 2, 2)], fsem.at[k, 0])
    lax.fori_loop(0, ng * PAIR_MOST, shrink(down_f, own), 0)

    for zz in range(nz):
        for xx in range(nx):
            S[xx, zz] = part[pl.ds((zz * nx + xx) * 24, 24), :]
    for k in range(1, nx):
        peer = lax.rem(x + k, nx)
        remote(S.at[peer], pbuf.at[x], p1.at[nx - k], g, z * nx + peer)

    def finish_x(dz):
        for k in range(1, nx // 2 + 1):
            wave("B", "x", k, dz)

    def a_wave(k):
        for dx in range(nx):
            wave("A", "z", k, dx)

    finish_x(0)

    pbuf[pl.ds(x, 1)] = S[pl.ds(x, 1)]
    for k in range(1, nx):
        arrived(pbuf.at[lax.rem(x + k, nx)], p1.at[k])
    total = pbuf[0]
    for xx in range(1, nx):
        total = total + pbuf[xx]
    pbuf[0] = total
    for k in range(1, nz):
        peer = lax.rem(z + k, nz)
        remote(pbuf.at[0, peer], sbuf.at[z], p2.at[nz - k], g, peer * nx + x)

    if nz > 1:
        a_wave(1)

    sbuf[pl.ds(z, 1)] = pbuf[0, pl.ds(z, 1)]
    for k in range(1, nz):
        arrived(sbuf.at[lax.rem(z + k, nz)], p2.at[k])
    low = sbuf[0]
    for zz in range(1, nz):
        low = low + sbuf[zz]
    low = jnp.concatenate([low, jnp.zeros((8, 128), F32)], axis=0).astype(BF16)
    lrz[pl.ds(z, 1)] = low[None]
    for k in range(1, nz):
        peer = lax.rem(z + k, nz)
        remote(lrz.at[z], lrz.at[z], p3.at[nz - k], g, peer * nx + x)

    for load in loads[4:6]:
        load.wait()

    kt = 512

    def base_of(dz):
        rows = pl.ds(pl.multiple_of(lax.rem(z + dz % nz, nz) * (nx * 48), 16), nx * 48)
        acc[...] = jnp.zeros(acc.shape, F32)

        def body(k, carry):
            cols = pl.ds(pl.multiple_of(k * kt, kt), kt)
            for h in range(2):
                acc[h] += jnp.dot(X[rows, cols], wv[h, cols, :], preferred_element_type=F32)
            return carry

        lax.fori_loop(0, K2 // kt, body, 0)
        first = acc[0].reshape(nx * 3, 2, 8, NW)[:, 0]
        second = acc[1].reshape(nx * 3, 2, 8, NW)[:, 1]
        return (first + second).reshape(nx * 24, NW)

    def finish(dz):
        base = base_of(dz)
        zz = lax.rem(z + dz % nz, nz)
        rows = pl.ds(pl.multiple_of(zz * (nx * 24), 8), nx * 24)
        query = base[:, :256] + adapter_scale * Dq[rows, :]
        keyval = base[:, 256:320] + adapter_scale * Dv[rows, :][:, :64]
        for xx in range(nx):
            q = query[xx * 24 : xx * 24 + 24]
            kv = keyval[xx * 24 : xx * 24 + 24]
            block = jnp.concatenate(
                [
                    q[:, :128], q[:, 128:],
                    jnp.concatenate([kv[0:8], kv[8:16]], axis=-1),
                    jnp.concatenate([kv[16:24], jnp.zeros((8, 64), F32)], axis=-1),
                ],
                axis=0,
            )
            ob[dz % nz, xx] = block.astype(BF16)
        for dx in range(nx):
            xx = lax.rem(x + dx, nx)
            if dx == 0 and dz % nz == 0:
                keep = pltpu.make_async_copy(ob.at[0, xx], out.at[t], wsem.at[8])
                keep.start()
                keep.wait()
            else:
                remote(ob.at[dz % nz, xx], out.at[t], osem.at[(-dx) % nx, (-dz) % nz], g, zz * nx + xx)

    for k in range(1, nz):
        arrived(lrz.at[lax.rem(z + k, nz)], p3.at[k])
    lrall[pl.ds(x, 1)] = lrz[...][None]
    for k in range(1, nx):
        peer = lax.rem(x + k, nx)
        remote(lrz, lrall.at[x], p4.at[nx - k], g, z * nx + peer)

    for k in range(1, nx):
        arrived(lrall.at[lax.rem(x + k, nx)], p4.at[k])
    for k in range(1, ng):
        peer = lax.rem(g + k, ng)
        for j in range(PAIR_MOST):
            spot = pl.ds(pl.multiple_of((peer * 2 + j) * rank, 16), rank)
            arrived(q_f.at[spot, :], fsem.at[k, 1 + j])
            arrived(v_f.at[spot, :], fsem.at[k, 3 + j])

    for zz in range(nz):
        for xx in range(nx):
            low24 = lrall[xx, zz].astype(F32)[:24]
            spot = pl.ds((zz * nx + xx) * 24, 24)
            LRq[spot, :] = jnp.concatenate([low24[:, :64], low24[:, :64]], axis=-1)
            LRv[spot, :] = jnp.concatenate([low24[:, 64:], low24[:, 64:]], axis=-1)
    Dq[...] = jnp.zeros(Dq.shape, F32)
    Dv[...] = jnp.zeros(Dv.shape, F32)

    def grow(q_table, v_table, first):
        def body(i, carry):
            lane = lax.broadcasted_iota(jnp.int32, (nt * 24, 128), 1) // 64
            hit0 = tr[...] == lane + (i * 4 + first)
            hit1 = tr[...] == lane + (i * 4 + 2 + first)
            spread_q = jnp.concatenate([jnp.where(hit0, LRq[...], 0.0), jnp.where(hit1, LRq[...], 0.0)], axis=-1)
            spread_v = jnp.concatenate([jnp.where(hit0, LRv[...], 0.0), jnp.where(hit1, LRv[...], 0.0)], axis=-1)
            Dq[...] += jnp.dot(spread_q.astype(BF16), q_table(i), preferred_element_type=F32)
            Dv[...] += jnp.dot(spread_v.astype(BF16), v_table(i), preferred_element_type=F32)
            return carry
        return body

    def own_table(ref):
        return lambda i: ref[pl.ds(i * 4, 4)].reshape(4 * rank, ref.shape[2])

    def far_table(ref):
        return lambda i: ref[pl.ds(pl.multiple_of(i * 4 * rank, 4 * rank), 4 * rank), :]

    lax.fori_loop(0, own // 4, grow(own_table(q_o), own_table(v_o), 0), 0)
    lax.fori_loop(0, ng * PAIR_MOST // 4, grow(far_table(q_f), far_table(v_f), own), 0)

    finish(0)
    for k in range(1, nz // 2 + 1):
        if k > 1:
            a_wave(k)
        for sign in ((-1, 1) if k < nz // 2 else (1,)):
            finish_x(sign * k)
            finish(sign * k)

    for dz in range(nz):
        for dx in range(nx):
            if dx or dz:
                arrived(out.at[dev(dx, dz)], osem.at[dx, dz])
    for copy in pending:
        copy.wait_send()


def project(nx, nz, ng, xk, xl, w, down, qup, vup, req, tr):
    nt = nx * nz
    K2 = xk.shape[1]
    own = down.shape[0]
    NW = w.shape[1]
    DMA = pltpu.SemaphoreType.DMA
    vmem = pl.BlockSpec(memory_space=pltpu.VMEM)
    hbm = pl.BlockSpec(memory_space=pl.ANY)
    sends = (nt - 1) + (ng - 1) * 6 + 5 * nt + 2 * (nx + nz) + 64 + nt + 160
    rows = nt * 24
    return pl.pallas_call(
        functools.partial(project_kernel, nx, nz, ng, own),
        out_shape=jax.ShapeDtypeStruct((nt, 64, 128), BF16),
        in_specs=[vmem, vmem, hbm, hbm, hbm, hbm, vmem, vmem],
        out_specs=vmem,
        scratch_shapes=[
            pltpu.VMEM((nt * 48, K2), BF16),
            pltpu.VMEM((2, K2, NW), BF16),
            pltpu.VMEM((nt * 48, 128), BF16),
            pltpu.VMEM((rows, 256), F32),
            pltpu.VMEM(down.shape, BF16),
            pltpu.VMEM(qup.shape, BF16),
            pltpu.VMEM(vup.shape, BF16),
            pltpu.VMEM((ng * 2,) + down.shape[1:], BF16),
            pltpu.VMEM((ng * 2 * 64, 256), BF16),
            pltpu.VMEM((ng * 2 * 64, 128), BF16),
            pltpu.VMEM((ng, 2) + down.shape[1:], BF16),
            pltpu.VMEM((ng, 2, 64, 256), BF16),
            pltpu.VMEM((ng, 2, 64, 128), BF16),
            pltpu.VMEM((ng, 8, 128), jnp.int32),
            pltpu.SMEM((ng, 8, 128), jnp.int32),
            pltpu.VMEM((rows, 128), F32),
            pltpu.VMEM((nx, nz, 24, 128), F32),
            pltpu.VMEM((nx, nz, 24, 128), F32),
            pltpu.VMEM((nz, 24, 128), F32),
            pltpu.VMEM((nz, 32, 128), BF16),
            pltpu.VMEM((nx, nz, 32, 128), BF16),
            pltpu.VMEM((rows, 128), F32),
            pltpu.VMEM((rows, 128), F32),
            pltpu.VMEM((rows, 256), F32),
            pltpu.VMEM((rows, 128), F32),
            pltpu.VMEM((2, nx * 48, NW), F32),
            pltpu.VMEM((nz, nx, 64, 128), BF16),
            DMA((sends,)),
            DMA((2, nx, nz, 2)),
            DMA((nt,)),
            DMA((1,)),
            DMA((ng, 5)),
            DMA((ng,)),
            DMA((nx,)),
            DMA((nz,)),
            DMA((nz,)),
            DMA((nx,)),
            DMA((nx, nz)),
            DMA((9,)),
        ],
        compiler_params=pltpu.CompilerParams(
            collective_id=0, has_side_effects=True, vmem_limit_bytes=56 * MIB
        ),
        name="project",
    )(xk, xl, w, down, qup, vup, req, tr)


def attend_kernel(lengths, q, fk, fv, hist, out):
    row = pl.program_id(0)
    window = hist.shape[1]
    kv_width = hist.shape[2] // 2
    length = lengths[row]
    factor = HEAD_DIM ** (-0.5)
    past_live = lax.broadcasted_iota(jnp.int32, (32, window), 1) < length
    step = lax.broadcasted_iota(jnp.int32, (32, 16), 0) // 8
    fresh_at = lax.broadcasted_iota(jnp.int32, (32, 16), 1)
    fresh_live = jnp.logical_and(fresh_at <= step, fresh_at < 3)
    for h in range(KV_HEADS):
        keys = hist[0, :, h * HEAD_DIM : (h + 1) * HEAD_DIM]
        values = hist[0, :, kv_width + h * HEAD_DIM : kv_width + (h + 1) * HEAD_DIM]
        queries = q[0, h]
        dims = (((1,), (1,)), ((), ()))
        past = lax.dot_general(queries, keys, dims, preferred_element_type=F32) * factor
        fresh = lax.dot_general(queries, fk[0, h], dims, preferred_element_type=F32) * factor
        past = jnp.where(past_live, past, -jnp.inf)
        fresh = jnp.where(fresh_live, fresh, -jnp.inf)
        highest = jnp.maximum(
            jnp.max(past, axis=-1, keepdims=True), jnp.max(fresh, axis=-1, keepdims=True)
        )
        past = jnp.exp(past - highest)
        fresh = jnp.exp(fresh - highest)
        total = jnp.sum(past, axis=-1, keepdims=True) + jnp.sum(fresh, axis=-1, keepdims=True)
        past = (past / total).astype(BF16)
        fresh = (fresh / total).astype(BF16)
        context = jnp.dot(past, values, preferred_element_type=F32) + jnp.dot(
            fresh, fv[0, h], preferred_element_type=F32
        )
        out[0, h] = context.astype(BF16)


def attend(lengths, q, fk, fv, hist):
    rows, window, width = hist.shape
    return pl.pallas_call(
        attend_kernel,
        out_shape=jax.ShapeDtypeStruct((rows, KV_HEADS, 32, HEAD_DIM), BF16),
        grid=(rows,),
        in_specs=[
            pl.BlockSpec(memory_space=pltpu.SMEM),
            pl.BlockSpec((1, KV_HEADS, 32, HEAD_DIM), lambda r: (r, 0, 0, 0)),
            pl.BlockSpec((1, KV_HEADS, 16, HEAD_DIM), lambda r: (r, 0, 0, 0)),
            pl.BlockSpec((1, KV_HEADS, 16, HEAD_DIM), lambda r: (r, 0, 0, 0)),
            pl.BlockSpec((1, window, width), lambda r: (r, 0, 0)),
        ],
        out_specs=pl.BlockSpec((1, KV_HEADS, 32, HEAD_DIM), lambda r: (r, 0, 0, 0)),
        compiler_params=pltpu.CompilerParams(vmem_limit_bytes=32 * MIB),
        name="attend",
    )(lengths, q, fk, fv, hist)


def routing(adapter_slot, row_adapter, store, groups, home):
    slots = adapter_slot.shape[0]
    catalog = jnp.arange(slots, dtype=jnp.int32)
    by_adapter = row_adapter[:, None] == catalog[None, :]
    slot_of_row = jnp.sum(jnp.where(by_adapter, adapter_slot[None, :], 0), axis=1)
    by_slot = slot_of_row[:, None] == catalog[None, :]
    source = slot_of_row // store
    offset = slot_of_row % store
    wanted = jnp.any(by_slot, axis=0).reshape(groups, store)
    foreign = jnp.logical_and(wanted, jnp.arange(groups, dtype=jnp.int32)[:, None] != home)
    marked = foreign.astype(jnp.int32)
    ranking = jnp.cumsum(marked, axis=1) - marked
    chosen = jnp.logical_and(
        foreign[:, :, None],
        ranking[:, :, None] == jnp.arange(PAIR_MOST, dtype=jnp.int32)[None, None, :],
    )
    request = jnp.sum(
        jnp.where(chosen, jnp.arange(store, dtype=jnp.int32)[None, :, None], 0), axis=1
    )
    row_rank = jnp.sum(jnp.where(by_slot, ranking.reshape(-1)[None, :], 0), axis=1)
    table_row = jnp.where(source == home, offset, store + source * PAIR_MOST + row_rank)
    return request, table_row


def projected(
    inputs, norm_gain, united_weight, adapter_down, query_up, value_up, adapter_slot, row_adapter
):
    steps, rows_here, width = inputs.shape
    nt = lax.axis_size("tensor")
    ng = lax.axis_size("group")
    nx = NX
    nz = nt // nx
    g = lax.axis_index("group")
    half = width // 2
    request, table_row = routing(adapter_slot, row_adapter, adapter_down.shape[0], ng, g)
    normed = rms_normed(inputs, norm_gain)
    xk = normed.reshape(steps, rows_here, 2, half).transpose(0, 2, 1, 3).reshape(steps * 2 * rows_here, half)
    xl = normed.reshape(steps * rows_here, nt * 2, 128).transpose(1, 0, 2).reshape(nt * 48, 128)
    req = jnp.pad(request[:, None, :], ((0, 0), (0, 7), (0, 128 - PAIR_MOST)))
    tr = jnp.broadcast_to(table_row.reshape(nt, 1, rows_here, 1), (nt, steps, rows_here, 128))
    tr = tr.reshape(nt * steps * rows_here, 128)
    vpad = jnp.pad(value_up, ((0, 0), (0, 0), (32, 64)))
    return project(nx, nz, ng, xk, xl, united_weight, adapter_down, query_up, vpad, req, tr)


def local(
    inputs, norm_gain, united_weight, adapter_down, query_up, value_up, history,
    adapter_slot, row_adapter, cache_length,
):
    steps, rows_here, width = inputs.shape
    nt = lax.axis_size("tensor")
    t = lax.axis_index("tensor")
    got = projected(
        inputs, norm_gain, united_weight, adapter_down, query_up, value_up, adapter_slot, row_adapter
    )
    lengths = lax.dynamic_slice_in_dim(cache_length, t * rows_here, rows_here, 0)
    query = got[:, :48].reshape(nt, 2, steps, rows_here, HEAD_DIM)
    query = query.transpose(2, 3, 0, 1, 4).reshape(steps, rows_here, HEADS, HEAD_DIM)
    fresh = got[:, 48:].reshape(nt, 2, rows_here, 2, 64).transpose(0, 2, 1, 3, 4)
    fresh = fresh.reshape(nt, rows_here, 4, 64)[:, :, :steps].transpose(2, 1, 0, 3)
    key = fresh[..., :32].reshape(steps, rows_here, KV_HEADS, HEAD_DIM)
    value = fresh[..., 32:].reshape(steps, rows_here, KV_HEADS, HEAD_DIM)
    positions = lengths[None, :] + jnp.arange(steps, dtype=jnp.int32)[:, None]
    query = rotate(query, positions)
    key = rotate(key, positions)
    q = query.reshape(steps, rows_here, KV_HEADS, HEADS // KV_HEADS, HEAD_DIM)
    q = q.transpose(1, 2, 0, 3, 4).reshape(rows_here, KV_HEADS, 24, HEAD_DIM)
    q = jnp.pad(q, ((0, 0), (0, 0), (0, 8), (0, 0)))
    fk = jnp.pad(key.transpose(1, 2, 0, 3), ((0, 0), (0, 0), (0, 13), (0, 0)))
    fv = jnp.pad(value.transpose(1, 2, 0, 3), ((0, 0), (0, 0), (0, 13), (0, 0)))
    context = attend(lengths, q, fk, fv, history)
    context = context[:, :, :24].reshape(rows_here, KV_HEADS, steps, HEADS // KV_HEADS, HEAD_DIM)
    return context.transpose(2, 0, 1, 3, 4).reshape(steps, rows_here, width)


def solution(mesh):
    in_specs = (
        P(None, ("group", "tensor"), None),
        P(),
        P(None, "tensor"),
        P("group", "tensor", None),
        P("group", None, "tensor"),
        P("group", None, "tensor"),
        P(("group", "tensor"), None, None),
        P(),
        P("group"),
        P("group"),
    )
    out_specs = P(None, ("group", "tensor"), None)
    return jax.shard_map(local, mesh=mesh, in_specs=in_specs, out_specs=out_specs, check_vma=False)
```

```python
import functools
import heapq

import jax
import jax.numpy as jnp
from jax import lax
from jax.experimental import pallas as pl
from jax.experimental.pallas import tpu as pltpu
from jax.sharding import PartitionSpec as P

HEADS = 64
KV_HEADS = 8
HEAD_DIM = 128
PAIR_MOST = 2
NX = 4

adapter_scale = 0.5
rope_base = 500000.0
norm_eps = 1e-05
MIB = 1024 * 1024
F32 = jnp.float32
BF16 = jnp.bfloat16
MESH = pl.DeviceIdType.MESH


def rms_normed(inputs, norm_gain):
    values = inputs.astype(F32)
    mean_square = jnp.mean(values * values, axis=-1, keepdims=True)
    return (values * lax.rsqrt(mean_square + norm_eps) * norm_gain.astype(F32)).astype(BF16)


def rotate(heads_in, positions):
    head_width = heads_in.shape[-1]
    halfway = head_width // 2
    ladder = jnp.arange(halfway).astype(F32) * (2.0 / head_width)
    inverse = jnp.power(F32(rope_base), -ladder)
    angles = positions.astype(F32)[..., None, None] * inverse
    cosine = jnp.cos(angles)
    sine_part = jnp.sin(angles)
    values = heads_in.astype(F32)
    leading = values[..., :halfway]
    trailing = values[..., halfway:]
    turned = jnp.concatenate(
        [leading * cosine - trailing * sine_part, trailing * cosine + leading * sine_part], axis=-1
    )
    return turned.astype(BF16)


CHORES = (3.0, 18.0, 50.0, 57.0, 63.0, 68.0, 73.0)
BUSY = {"x": 4.0, "z": 8.0}
RATE = 45e3


def ring_order(nx, nz, la, lb):
    sizes = {"A": la * 96 / RATE, "B": lb * 96 / RATE}
    span = {"x": nx, "z": nz}
    free = {(axis, step): BUSY[axis] for axis in "xz" for step in (1, -1)}
    heap = []
    halves = {}
    out = []
    count = [0]

    def send(now, name, dx, dz, half, axis, step):
        key = (axis, step)
        start = max(free[key], now)
        free[key] = start + sizes[name] * (1.0 if half is None else 0.5)
        out.append(("send", key, name, dx % nx, dz % nz, half))
        ndx = (dx - (step if axis == "x" else 0)) % nx
        ndz = (dz - (step if axis == "z" else 0)) % nz
        count[0] += 1
        heapq.heappush(heap, (free[key] + 1.5, count[0], name, ndx, ndz, half, axis, step))

    def launch(now, name, dx, dz, axis):
        if span[axis] > 2:
            send(now, name, dx, dz, None, axis, 1)
            send(now, name, dx, dz, None, axis, -1)
        elif span[axis] == 2:
            send(now, name, dx, dz, 0, axis, 1)
            send(now, name, dx, dz, 1, axis, -1)

    launch(0.0, "A", 0, 0, "x")
    launch(0.0, "B", 0, 0, "z")
    launch(0.0, "B", 0, 0, "x")
    launch(0.0, "A", 0, 0, "z")
    while heap:
        now, _, name, dx, dz, half, axis, step = heapq.heappop(heap)
        tie = (name, dx, dz)
        seen = halves.get(tie, 0)
        halves[tie] = seen + 1
        last = half is None or seen == 1
        out.append(("wait", now, name, dx, dz, half if half is None else (half, last)))
        size = span[axis]
        far = (-step * (dx if axis == "x" else dz)) % size
        if half is None:
            if far + 1 < size // 2:
                send(now, name, dx, dz, None, axis, step)
            elif far + 1 == size // 2:
                send(now, name, dx, dz, 0 if step > 0 else 1, axis, step)
        if last:
            if name == "A" and axis == "x":
                launch(now, name, dx, dz, "z")
            if name == "B" and axis == "z":
                launch(now, name, dx, dz, "x")
    return out


def project_kernel(
    nx, nz, ng, own,
    xk, xl, w, down, qup, vup, req, tr,
    out,
    X, wv, lbuf, xs, down_o, q_o, v_o, down_f, q_f, v_f, sd, sq, sv, rbuf, rs,
    part, pbuf, S, sbuf, lrz, lrall, LRq, LRv, Dq, Dv, acc, plain, ob,
    ssem, gsem, lsem, dsem, fsem, qsem, p1, p2, p3, p4, osem, wsem,
):
    nt = nx * nz
    K2 = X.shape[1]
    NW = w.shape[0]
    rank = 64
    tiles = K2 // 128
    ta = max((tiles * 12) // 32, 2)
    LA = ta * 128
    LB = K2 - LA
    spans = {
        "A": ((0, (ta // 2) * 128), ((ta // 2) * 128, LA - (ta // 2) * 128)),
        "B": ((LA, ((tiles - ta) // 2) * 128), (LA + ((tiles - ta) // 2) * 128, LB - ((tiles - ta) // 2) * 128)),
    }
    whole = {"A": (0, LA), "B": (LA, LB)}
    which = {"A": 0, "B": 1}

    g = lax.axis_index("group")
    t = lax.axis_index("tensor")
    z = t // nx
    x = t % nx

    def dev(dx, dz):
        return lax.rem(z + (dz % nz), nz) * nx + lax.rem(x + (dx % nx), nx)

    pending = []
    counter = [0]

    def remote(src, dst, rsem, group, tensor):
        sem = ssem.at[counter[0]]
        counter[0] += 1
        copy = pltpu.make_async_remote_copy(
            src_ref=src, dst_ref=dst, send_sem=sem, recv_sem=rsem,
            device_id=(group, tensor), device_id_type=MESH,
        )
        copy.start()
        pending.append(copy)

    def arrived(ref, sem):
        pltpu.make_async_copy(ref, ref, sem).wait()

    barrier = pltpu.get_barrier_semaphore()

    def greet(k, carry):
        pl.semaphore_signal(barrier, inc=1, device_id=(g, lax.rem(t + k, nt)), device_id_type=MESH)
        return carry

    lax.fori_loop(1, nt, greet, 0)

    def greet_group(k, carry):
        pl.semaphore_signal(barrier, inc=1, device_id=(lax.rem(g + k, ng), t), device_id_type=MESH)
        return carry

    lax.fori_loop(1, ng, greet_group, 0)

    mine = pl.multiple_of(t * 48, 16)
    loads = [
        pltpu.make_async_copy(xk, X.at[pl.ds(mine, 48), :], wsem.at[0]),
        pltpu.make_async_copy(down, down_o, wsem.at[1]),
        pltpu.make_async_copy(qup, q_o, wsem.at[2]),
        pltpu.make_async_copy(vup, v_o, wsem.at[3]),
        pltpu.make_async_copy(w.at[:, pl.ds(0, K2)], wv.at[0], wsem.at[4]),
        pltpu.make_async_copy(w.at[:, pl.ds(K2, K2)], wv.at[1], wsem.at[5]),
        pltpu.make_async_copy(xl.at[pl.ds(mine, 48), :], lbuf.at[pl.ds(mine, 48), :], wsem.at[6]),
    ]
    for load in loads:
        load.start()
    loads[0].wait()

    pl.semaphore_wait(barrier, nt - 1 + ng - 1)

    def piece(dx, dz, lo, n):
        rows = pl.multiple_of(dev(dx, dz) * 48, 16)
        return X.at[pl.ds(rows, 48), pl.ds(lo, n)]

    def forward(name, dx, dz, half, axis, step):
        lo, n = whole[name] if half is None else spans[name][half]
        ref = piece(dx, dz, lo, n)
        if axis == "x":
            there = dev(step, 0)
            ndx, ndz = (dx - step) % nx, dz % nz
        else:
            there = dev(0, step)
            ndx, ndz = dx % nx, (dz - step) % nz
        remote(ref, ref, gsem.at[which[name], ndx, ndz, 0 if half is None else half], g, there)

    def expect(name, dx, dz, half):
        lo, n = whole[name] if half is None else spans[name][half]
        arrived(piece(dx, dz, lo, n), gsem.at[which[name], dx % nx, dz % nz, 0 if half is None else half])

    for k in range(1, nt):
        peer = lax.rem(t + k, nt)
        remote(
            xl.at[pl.ds(pl.multiple_of(peer * 48, 16), 48), :],
            lbuf.at[pl.ds(mine, 48), :], lsem.at[nt - k], g, peer,
        )
    for k in range(1, ng):
        peer = lax.rem(g + k, ng)
        remote(req.at[peer], rbuf.at[g], qsem.at[ng - k], peer, t)

    def lend():
        for load in loads[1:4]:
            load.wait()
        down_f[pl.ds(g * 2, 2)] = jnp.zeros((2,) + down_f.shape[1:], BF16)
        own_spot = pl.ds(pl.multiple_of(g * 2 * rank, 16), 2 * rank)
        q_f[own_spot, :] = jnp.zeros((2 * rank, q_f.shape[1]), BF16)
        v_f[own_spot, :] = jnp.zeros((2 * rank, v_f.shape[1]), BF16)
        for k in range(1, ng):
            peer = lax.rem(g + k, ng)
            arrived(rbuf.at[peer], qsem.at[k])
            down_copy = pltpu.make_async_copy(rbuf.at[peer], rs.at[k], wsem.at[7])
            down_copy.start()
            down_copy.wait()
            for j in range(PAIR_MOST):
                slot = rs[k, 0, j]
                sd[k, j] = down_o[slot]
                sq[k, j] = q_o[slot]
                sv[k, j] = v_o[slot]
            remote(sd.at[k], down_f.at[pl.ds(g * 2, 2)], fsem.at[ng - k, 0], peer, t)
            for j in range(PAIR_MOST):
                spot = pl.ds(pl.multiple_of((g * 2 + j) * rank, 16), rank)
                remote(sq.at[k, j], q_f.at[spot, :], fsem.at[ng - k, 1 + j], peer, t)
                remote(sv.at[k, j], v_f.at[spot, :], fsem.at[ng - k, 3 + j], peer, t)

    def shrink(table, first):
        def body(e, carry):
            chosen = tr[...] == e + first
            pick = jnp.concatenate([chosen, chosen], axis=-1)
            rows = jnp.where(pick, xs[...], 0.0).astype(BF16)
            part[...] += jnp.dot(rows, table[e], preferred_element_type=F32)
            return carry
        return body

    def shrink_own():
        loads[6].wait()
        for k in range(1, nt):
            arrived(lbuf.at[pl.ds(pl.multiple_of(lax.rem(t + k, nt) * 48, 16), 48), :], lsem.at[k])
        both = lbuf[...].astype(F32).reshape(nt, 2, 24, 128)
        xs[...] = jnp.concatenate([both[:, 0], both[:, 1]], axis=-1).reshape(nt * 24, 256)
        part[...] = jnp.zeros(part.shape, F32)
        lax.fori_loop(0, own, shrink(down_o, 0), 0)

    def shrink_far():
        for k in range(1, ng):
            peer = lax.rem(g + k, ng)
            arrived(down_f.at[pl.ds(peer * 2, 2)], fsem.at[k, 0])
        lax.fori_loop(0, ng * PAIR_MOST, shrink(down_f, own), 0)
        for zz in range(nz):
            for xx in range(nx):
                S[xx, zz] = part[pl.ds((zz * nx + xx) * 24, 24), :]
        for k in range(1, nx):
            peer = lax.rem(x + k, nx)
            remote(S.at[peer], pbuf.at[x], p1.at[nx - k], g, z * nx + peer)

    def sum_x():
        pbuf[pl.ds(x, 1)] = S[pl.ds(x, 1)]
        for k in range(1, nx):
            arrived(pbuf.at[lax.rem(x + k, nx)], p1.at[k])
        total = pbuf[0]
        for xx in range(1, nx):
            total = total + pbuf[xx]
        pbuf[0] = total
        for k in range(1, nz):
            peer = lax.rem(z + k, nz)
            remote(pbuf.at[0, peer], sbuf.at[z], p2.at[nz - k], g, peer * nx + x)

    def sum_z():
        sbuf[pl.ds(z, 1)] = pbuf[0, pl.ds(z, 1)]
        for k in range(1, nz):
            arrived(sbuf.at[lax.rem(z + k, nz)], p2.at[k])
        low = sbuf[0]
        for zz in range(1, nz):
            low = low + sbuf[zz]
        low = jnp.concatenate([low, jnp.zeros((8, 128), F32)], axis=0).astype(BF16)
        lrz[pl.ds(z, 1)] = low[None]
        for k in range(1, nz):
            peer = lax.rem(z + k, nz)
            remote(lrz.at[z], lrz.at[z], p3.at[nz - k], g, peer * nx + x)

    def spread_x():
        for k in range(1, nz):
            arrived(lrz.at[lax.rem(z + k, nz)], p3.at[k])
        lrall[pl.ds(x, 1)] = lrz[...][None]
        for k in range(1, nx):
            peer = lax.rem(x + k, nx)
            remote(lrz, lrall.at[x], p4.at[nx - k], g, z * nx + peer)

    def expand():
        for k in range(1, nx):
            arrived(lrall.at[lax.rem(x + k, nx)], p4.at[k])
        for k in range(1, ng):
            peer = lax.rem(g + k, ng)
            for j in range(PAIR_MOST):
                spot = pl.ds(pl.multiple_of((peer * 2 + j) * rank, 16), rank)
                arrived(q_f.at[spot, :], fsem.at[k, 1 + j])
                arrived(v_f.at[spot, :], fsem.at[k, 3 + j])

        for zz in range(nz):
            for xx in range(nx):
                low24 = lrall[xx, zz].astype(F32)[:24]
                spot = pl.ds((zz * nx + xx) * 24, 24)
                LRq[spot, :] = jnp.concatenate([low24[:, :64], low24[:, :64]], axis=-1)
                LRv[spot, :] = jnp.concatenate([low24[:, 64:], low24[:, 64:]], axis=-1)
        Dq[...] = jnp.zeros(Dq.shape, F32)
        Dv[...] = jnp.zeros(Dv.shape, F32)

        def grow(q_table, v_table, first):
            def body(i, carry):
                lane = lax.broadcasted_iota(jnp.int32, (nt * 24, 128), 1) // 64
                hit0 = tr[...] == lane + (i * 4 + first)
                hit1 = tr[...] == lane + (i * 4 + 2 + first)
                spread_q = jnp.concatenate([jnp.where(hit0, LRq[...], 0.0), jnp.where(hit1, LRq[...], 0.0)], axis=-1)
                spread_v = jnp.concatenate([jnp.where(hit0, LRv[...], 0.0), jnp.where(hit1, LRv[...], 0.0)], axis=-1)
                Dq[...] += jnp.dot(spread_q.astype(BF16), q_table(i), preferred_element_type=F32)
                Dv[...] += jnp.dot(spread_v.astype(BF16), v_table(i), preferred_element_type=F32)
                return carry
            return body

        def own_table(ref):
            return lambda i: ref[pl.ds(i * 4, 4)].reshape(4 * rank, ref.shape[2])

        def far_table(ref):
            return lambda i: ref[pl.ds(pl.multiple_of(i * 4 * rank, 4 * rank), 4 * rank), :]

        lax.fori_loop(0, own // 4, grow(own_table(q_o), own_table(v_o), 0), 0)
        lax.fori_loop(0, ng * PAIR_MOST // 4, grow(far_table(q_f), far_table(v_f), own), 0)

    kt = 512

    def base_of(dz):
        rows = pl.ds(pl.multiple_of(lax.rem(z + dz % nz, nz) * (nx * 48), 16), nx * 48)
        acc[...] = jnp.zeros(acc.shape, F32)

        def body(k, carry):
            cols = pl.ds(pl.multiple_of(k * kt, kt), kt)
            for h in range(2):
                acc[h] += lax.dot_general(
                    X[rows, cols], wv[h, :, cols], (((1,), (1,)), ((), ())), preferred_element_type=F32
                )
            return carry

        lax.fori_loop(0, K2 // kt, body, 0)
        first = acc[0].reshape(nx * 3, 2, 8, NW)[:, 0]
        second = acc[1].reshape(nx * 3, 2, 8, NW)[:, 1]
        plain[dz % nz] = (first + second).reshape(nx * 24, NW)

    def finish(dz):
        base = plain[dz % nz]
        zz = lax.rem(z + dz % nz, nz)
        rows = pl.ds(pl.multiple_of(zz * (nx * 24), 8), nx * 24)
        query = base[:, :256] + adapter_scale * Dq[rows, :]
        keyval = base[:, 256:320] + adapter_scale * Dv[rows, :][:, :64]
        for xx in range(nx):
            q = query[xx * 24 : xx * 24 + 24]
            kv = keyval[xx * 24 : xx * 24 + 24]
            block = jnp.concatenate(
                [
                    q[:, :128], q[:, 128:],
                    jnp.concatenate([kv[0:8], kv[8:16]], axis=-1),
                    jnp.concatenate([kv[16:24], jnp.zeros((8, 64), F32)], axis=-1),
                ],
                axis=0,
            )
            ob[dz % nz, xx] = block.astype(BF16)
        for dx in range(nx):
            xx = lax.rem(x + dx, nx)
            if dx == 0 and dz % nz == 0:
                keep = pltpu.make_async_copy(ob.at[0, xx], out.at[t], wsem.at[8])
                keep.start()
                keep.wait()
            else:
                remote(ob.at[dz % nz, xx], out.at[t], osem.at[(-dx) % nx, (-dz) % nz], g, zz * nx + xx)

    chores = [
        (CHORES[0], lend), (CHORES[1], shrink_own), (CHORES[2], shrink_far), (CHORES[3], sum_x),
        (CHORES[4], sum_z), (CHORES[5], spread_x), (CHORES[6], expand),
    ]
    loaded = []
    ready = []
    based = []
    missing = {dz: 2 * nx for dz in range(nz)}
    missing[0] -= 2

    def settle(now):
        while chores and chores[0][0] <= now:
            chores.pop(0)[1]()
        while ready:
            if not loaded:
                for load in loads[4:6]:
                    load.wait()
                loaded.append(1)
            dz = ready.pop(0)
            base_of(dz)
            based.append(dz)
        while based and not chores:
            finish(based.pop(0))

    for kind, when, name, dx, dz, half in ring_order(nx, nz, LA, LB):
        if kind == "send":
            axis, step = when
            forward(name, dx, dz, half, axis, step)
        else:
            settle(when)
            piece_half, last = (None, True) if half is None else half
            expect(name, dx, dz, piece_half)
            if last:
                missing[dz] -= 1
                if missing[dz] == 0:
                    ready.append(dz)
    settle(1e9)

    for dz in range(nz):
        for dx in range(nx):
            if dx or dz:
                arrived(out.at[dev(dx, dz)], osem.at[dx, dz])
    for copy in pending:
        copy.wait_send()


def project(nx, nz, ng, xk, xl, w, down, qup, vup, req, tr):
    nt = nx * nz
    K2 = xk.shape[1]
    own = down.shape[0]
    NW = w.shape[0]
    DMA = pltpu.SemaphoreType.DMA
    vmem = pl.BlockSpec(memory_space=pltpu.VMEM)
    hbm = pl.BlockSpec(memory_space=pl.ANY)
    sends = (nt - 1) + (ng - 1) * 6 + 5 * nt + 2 * (nx + nz) + 64 + nt + 160
    rows = nt * 24
    return pl.pallas_call(
        functools.partial(project_kernel, nx, nz, ng, own),
        out_shape=jax.ShapeDtypeStruct((nt, 64, 128), BF16),
        in_specs=[vmem, vmem, hbm, hbm, hbm, hbm, vmem, vmem],
        out_specs=vmem,
        scratch_shapes=[
            pltpu.VMEM((nt * 48, K2), BF16),
            pltpu.VMEM((2, NW, K2), BF16),
            pltpu.VMEM((nt * 48, 128), BF16),
            pltpu.VMEM((rows, 256), F32),
            pltpu.VMEM(down.shape, BF16),
            pltpu.VMEM(qup.shape, BF16),
            pltpu.VMEM(vup.shape, BF16),
            pltpu.VMEM((ng * 2,) + down.shape[1:], BF16),
            pltpu.VMEM((ng * 2 * 64, 256), BF16),
            pltpu.VMEM((ng * 2 * 64, 128), BF16),
            pltpu.VMEM((ng, 2) + down.shape[1:], BF16),
            pltpu.VMEM((ng, 2, 64, 256), BF16),
            pltpu.VMEM((ng, 2, 64, 128), BF16),
            pltpu.VMEM((ng, 8, 128), jnp.int32),
            pltpu.SMEM((ng, 8, 128), jnp.int32),
            pltpu.VMEM((rows, 128), F32),
            pltpu.VMEM((nx, nz, 24, 128), F32),
            pltpu.VMEM((nx, nz, 24, 128), F32),
            pltpu.VMEM((nz, 24, 128), F32),
            pltpu.VMEM((nz, 32, 128), BF16),
            pltpu.VMEM((nx, nz, 32, 128), BF16),
            pltpu.VMEM((rows, 128), F32),
            pltpu.VMEM((rows, 128), F32),
            pltpu.VMEM((rows, 256), F32),
            pltpu.VMEM((rows, 128), F32),
            pltpu.VMEM((2, nx * 48, NW), F32),
            pltpu.VMEM((nz, nx * 24, NW), F32),
            pltpu.VMEM((nz, nx, 64, 128), BF16),
            DMA((sends,)),
            DMA((2, nx, nz, 2)),
            DMA((nt,)),
            DMA((1,)),
            DMA((ng, 5)),
            DMA((ng,)),
            DMA((nx,)),
            DMA((nz,)),
            DMA((nz,)),
            DMA((nx,)),
            DMA((nx, nz)),
            DMA((9,)),
        ],
        compiler_params=pltpu.CompilerParams(
            collective_id=0, has_side_effects=True, vmem_limit_bytes=56 * MIB
        ),
        name="project",
    )(xk, xl, w, down, qup, vup, req, tr)


def attend_kernel(lengths, q, fk, fv, hist, out):
    row = pl.program_id(0)
    window = hist.shape[1]
    kv_width = hist.shape[2] // 2
    length = lengths[row]
    factor = HEAD_DIM ** (-0.5)
    past_live = lax.broadcasted_iota(jnp.int32, (KV_HEADS * 32, window), 1) < length
    at = lax.broadcasted_iota(jnp.int32, (KV_HEADS * 32, KV_HEADS * 16), 0)
    fresh_at = lax.broadcasted_iota(jnp.int32, (KV_HEADS * 32, KV_HEADS * 16), 1)
    same_head = at // 32 == fresh_at // 16
    order = fresh_at % 16
    fresh_live = jnp.logical_and(same_head, jnp.logical_and(order <= (at % 32) // 8, order < 3))
    dims = (((1,), (1,)), ((), ()))
    past = []
    for h in range(KV_HEADS):
        keys = hist[0, :, h * HEAD_DIM : (h + 1) * HEAD_DIM]
        past.append(lax.dot_general(q[0, h], keys, dims, preferred_element_type=F32))
    past = jnp.concatenate(past, axis=0) * factor
    queries = q[0].reshape(KV_HEADS * 32, HEAD_DIM)
    fresh_keys = fk[0].reshape(KV_HEADS * 16, HEAD_DIM)
    fresh_values = fv[0].reshape(KV_HEADS * 16, HEAD_DIM)
    fresh = lax.dot_general(queries, fresh_keys, dims, preferred_element_type=F32) * factor
    past = jnp.where(past_live, past, -jnp.inf)
    fresh = jnp.where(fresh_live, fresh, -jnp.inf)
    highest = jnp.maximum(
        jnp.max(past, axis=-1, keepdims=True), jnp.max(fresh, axis=-1, keepdims=True)
    )
    past = jnp.exp(past - highest)
    fresh = jnp.exp(fresh - highest)
    total = jnp.sum(past, axis=-1, keepdims=True) + jnp.sum(fresh, axis=-1, keepdims=True)
    past = (past / total).astype(BF16)
    fresh = (fresh / total).astype(BF16)
    context = jnp.dot(fresh, fresh_values, preferred_element_type=F32)
    for h in range(KV_HEADS):
        values = hist[0, :, kv_width + h * HEAD_DIM : kv_width + (h + 1) * HEAD_DIM]
        rows = slice(h * 32, (h + 1) * 32)
        out[0, h] = (
            context[rows] + jnp.dot(past[rows], values, preferred_element_type=F32)
        ).astype(BF16)


def attend(lengths, q, fk, fv, hist):
    rows, window, width = hist.shape
    return pl.pallas_call(
        attend_kernel,
        out_shape=jax.ShapeDtypeStruct((rows, KV_HEADS, 32, HEAD_DIM), BF16),
        grid=(rows,),
        in_specs=[
            pl.BlockSpec(memory_space=pltpu.SMEM),
            pl.BlockSpec((1, KV_HEADS, 32, HEAD_DIM), lambda r: (r, 0, 0, 0)),
            pl.BlockSpec((1, KV_HEADS, 16, HEAD_DIM), lambda r: (r, 0, 0, 0)),
            pl.BlockSpec((1, KV_HEADS, 16, HEAD_DIM), lambda r: (r, 0, 0, 0)),
            pl.BlockSpec((1, window, width), lambda r: (r, 0, 0)),
        ],
        out_specs=pl.BlockSpec((1, KV_HEADS, 32, HEAD_DIM), lambda r: (r, 0, 0, 0)),
        compiler_params=pltpu.CompilerParams(vmem_limit_bytes=56 * MIB),
        name="attend",
    )(lengths, q, fk, fv, hist)


def routing(adapter_slot, row_adapter, store, groups, home):
    slots = adapter_slot.shape[0]
    catalog = jnp.arange(slots, dtype=jnp.int32)
    by_adapter = row_adapter[:, None] == catalog[None, :]
    slot_of_row = jnp.sum(jnp.where(by_adapter, adapter_slot[None, :], 0), axis=1)
    by_slot = slot_of_row[:, None] == catalog[None, :]
    source = slot_of_row // store
    offset = slot_of_row % store
    wanted = jnp.any(by_slot, axis=0).reshape(groups, store)
    foreign = jnp.logical_and(wanted, jnp.arange(groups, dtype=jnp.int32)[:, None] != home)
    marked = foreign.astype(jnp.int32)
    ranking = jnp.cumsum(marked, axis=1) - marked
    chosen = jnp.logical_and(
        foreign[:, :, None],
        ranking[:, :, None] == jnp.arange(PAIR_MOST, dtype=jnp.int32)[None, None, :],
    )
    request = jnp.sum(
        jnp.where(chosen, jnp.arange(store, dtype=jnp.int32)[None, :, None], 0), axis=1
    )
    row_rank = jnp.sum(jnp.where(by_slot, ranking.reshape(-1)[None, :], 0), axis=1)
    table_row = jnp.where(source == home, offset, store + source * PAIR_MOST + row_rank)
    return request, table_row


def projected(
    inputs, norm_gain, united_weight, adapter_down, query_up, value_up, adapter_slot, row_adapter
):
    steps, rows_here, width = inputs.shape
    nt = lax.axis_size("tensor")
    ng = lax.axis_size("group")
    nx = NX
    nz = nt // nx
    g = lax.axis_index("group")
    half = width // 2
    request, table_row = routing(adapter_slot, row_adapter, adapter_down.shape[0], ng, g)
    normed = rms_normed(inputs, norm_gain)
    xk = normed.reshape(steps, rows_here, 2, half).transpose(0, 2, 1, 3).reshape(steps * 2 * rows_here, half)
    xl = normed.reshape(steps * rows_here, nt * 2, 128).transpose(1, 0, 2).reshape(nt * 48, 128)
    req = jnp.pad(request[:, None, :], ((0, 0), (0, 7), (0, 128 - PAIR_MOST)))
    tr = jnp.broadcast_to(table_row.reshape(nt, 1, rows_here, 1), (nt, steps, rows_here, 128))
    tr = tr.reshape(nt * steps * rows_here, 128)
    vpad = jnp.pad(value_up, ((0, 0), (0, 0), (32, 64)))
    return project(nx, nz, ng, xk, xl, united_weight.T, adapter_down, query_up, vpad, req, tr)


def local(
    inputs, norm_gain, united_weight, adapter_down, query_up, value_up, history,
    adapter_slot, row_adapter, cache_length,
):
    steps, rows_here, width = inputs.shape
    nt = lax.axis_size("tensor")
    t = lax.axis_index("tensor")
    got = projected(
        inputs, norm_gain, united_weight, adapter_down, query_up, value_up, adapter_slot, row_adapter
    )
    lengths = lax.dynamic_slice_in_dim(cache_length, t * rows_here, rows_here, 0)
    query = got[:, :48].reshape(nt, 2, steps, rows_here, HEAD_DIM)
    query = query.transpose(2, 3, 0, 1, 4).reshape(steps, rows_here, HEADS, HEAD_DIM)
    fresh = got[:, 48:].reshape(nt, 2, rows_here, 2, 64).transpose(0, 2, 1, 3, 4)
    fresh = fresh.reshape(nt, rows_here, 4, 64)[:, :, :steps].transpose(2, 1, 0, 3)
    key = fresh[..., :32].reshape(steps, rows_here, KV_HEADS, HEAD_DIM)
    value = fresh[..., 32:].reshape(steps, rows_here, KV_HEADS, HEAD_DIM)
    positions = lengths[None, :] + jnp.arange(steps, dtype=jnp.int32)[:, None]
    query = rotate(query, positions)
    key = rotate(key, positions)
    q = query.reshape(steps, rows_here, KV_HEADS, HEADS // KV_HEADS, HEAD_DIM)
    q = q.transpose(1, 2, 0, 3, 4).reshape(rows_here, KV_HEADS, 24, HEAD_DIM)
    q = jnp.pad(q, ((0, 0), (0, 0), (0, 8), (0, 0)))
    fk = jnp.pad(key.transpose(1, 2, 0, 3), ((0, 0), (0, 0), (0, 13), (0, 0)))
    fv = jnp.pad(value.transpose(1, 2, 0, 3), ((0, 0), (0, 0), (0, 13), (0, 0)))
    context = attend(lengths, q, fk, fv, history)
    context = context[:, :, :24].reshape(rows_here, KV_HEADS, steps, HEADS // KV_HEADS, HEAD_DIM)
    return context.transpose(2, 0, 1, 3, 4).reshape(steps, rows_here, width)


def solution(mesh):
    in_specs = (
        P(None, ("group", "tensor"), None),
        P(),
        P(None, "tensor"),
        P("group", "tensor", None),
        P("group", None, "tensor"),
        P("group", None, "tensor"),
        P(("group", "tensor"), None, None),
        P(),
        P("group"),
        P("group"),
    )
    out_specs = P(None, ("group", "tensor"), None)
    return jax.shard_map(local, mesh=mesh, in_specs=in_specs, out_specs=out_specs, check_vma=False)
```

```python
import functools
import heapq

import jax
import jax.numpy as jnp
from jax import lax
from jax.experimental import pallas as pl
from jax.experimental.pallas import tpu as pltpu
from jax.sharding import PartitionSpec as P

HEADS = 64
KV_HEADS = 8
HEAD_DIM = 128
PAIR_MOST = 2
NX = 4

adapter_scale = 0.5
rope_base = 500000.0
norm_eps = 1e-05
MIB = 1024 * 1024
F32 = jnp.float32
BF16 = jnp.bfloat16
MESH = pl.DeviceIdType.MESH


def rope_tables(positions):
    halfway = HEAD_DIM // 2
    ladder = jnp.arange(halfway).astype(F32) * (2.0 / HEAD_DIM)
    inverse = jnp.power(F32(rope_base), -ladder)
    angles = positions.astype(F32)[:, None] * inverse[None, :]
    cosine = jnp.cos(angles)
    sine = jnp.sin(angles)
    return jnp.concatenate([cosine, cosine], axis=-1), jnp.concatenate([-sine, sine], axis=-1)


CHORES = (3.0, 16.0, 32.0, 46.0, 56.0, 66.0, 75.0)
BUSY = {"x": 4.0, "z": 8.0}
RATE = 45e3


def ring_order(nx, nz, la, lb):
    sizes = {"A": la * 96 / RATE, "B": lb * 96 / RATE}
    span = {"x": nx, "z": nz}
    free = {(axis, step): BUSY[axis] for axis in "xz" for step in (1, -1)}
    heap = []
    halves = {}
    out = []
    count = [0]

    def send(now, name, dx, dz, half, axis, step):
        key = (axis, step)
        start = max(free[key], now)
        free[key] = start + sizes[name] * (1.0 if half is None else 0.5)
        out.append(("send", key, name, dx % nx, dz % nz, half))
        ndx = (dx - (step if axis == "x" else 0)) % nx
        ndz = (dz - (step if axis == "z" else 0)) % nz
        count[0] += 1
        heapq.heappush(heap, (free[key] + 1.5, count[0], name, ndx, ndz, half, axis, step))

    def launch(now, name, dx, dz, axis):
        if span[axis] > 2:
            send(now, name, dx, dz, None, axis, 1)
            send(now, name, dx, dz, None, axis, -1)
        elif span[axis] == 2:
            send(now, name, dx, dz, 0, axis, 1)
            send(now, name, dx, dz, 1, axis, -1)

    launch(0.0, "A", 0, 0, "x")
    launch(0.0, "B", 0, 0, "z")
    launch(0.0, "B", 0, 0, "x")
    launch(0.0, "A", 0, 0, "z")
    while heap:
        now, _, name, dx, dz, half, axis, step = heapq.heappop(heap)
        tie = (name, dx, dz)
        seen = halves.get(tie, 0)
        halves[tie] = seen + 1
        last = half is None or seen == 1
        out.append(("wait", now, name, dx, dz, half if half is None else (half, last)))
        size = span[axis]
        far = (-step * (dx if axis == "x" else dz)) % size
        if half is None:
            if far + 1 < size // 2:
                send(now, name, dx, dz, None, axis, step)
            elif far + 1 == size // 2:
                send(now, name, dx, dz, 0 if step > 0 else 1, axis, step)
        if last:
            if name == "A" and axis == "x":
                launch(now, name, dx, dz, "z")
            if name == "B" and axis == "z":
                launch(now, name, dx, dz, "x")
    return out


def project_kernel(
    nx, nz, ng, own,
    inputs, gain, w, down, qup, vup, req, spot_of_row,
    out,
    X, xl, tr, wv, vraw, lbuf, xs, down_o, q_o, v_o, down_f, q_f, v_f, sd, sq, sv, rbuf, rsend, rs,
    part, pbuf, S, half_sum, sbuf, lrz, lrall, LRq, LRv, Dq, Dv, acc, plain, ob,
    ssem, gsem, lsem, dsem, fsem, qsem, p1, p2, p3, p4, osem, wsem,
):
    nt = nx * nz
    K2 = X.shape[1]
    NW = w.shape[0]
    rank = 64
    tiles = K2 // 128
    ta = max((tiles * 12) // 32, 2)
    LA = ta * 128
    LB = K2 - LA
    spans = {
        "A": ((0, (ta // 2) * 128), ((ta // 2) * 128, LA - (ta // 2) * 128)),
        "B": ((LA, ((tiles - ta) // 2) * 128), (LA + ((tiles - ta) // 2) * 128, LB - ((tiles - ta) // 2) * 128)),
    }
    whole = {"A": (0, LA), "B": (LA, LB)}
    which = {"A": 0, "B": 1}

    g = lax.axis_index("group")
    t = lax.axis_index("tensor")
    z = t // nx
    x = t % nx

    def dev(dx, dz):
        return lax.rem(z + (dz % nz), nz) * nx + lax.rem(x + (dx % nx), nx)

    pending = []
    counter = [0]

    def remote(src, dst, rsem, group, tensor):
        sem = ssem.at[counter[0]]
        counter[0] += 1
        copy = pltpu.make_async_remote_copy(
            src_ref=src, dst_ref=dst, send_sem=sem, recv_sem=rsem,
            device_id=(group, tensor), device_id_type=MESH,
        )
        copy.start()
        pending.append(copy)

    def arrived(ref, sem):
        pltpu.make_async_copy(ref, ref, sem).wait()

    barrier = pltpu.get_barrier_semaphore()

    def greet(k, carry):
        pl.semaphore_signal(barrier, inc=1, device_id=(g, lax.rem(t + k, nt)), device_id_type=MESH)
        return carry

    lax.fori_loop(1, nt, greet, 0)

    def greet_group(k, carry):
        pl.semaphore_signal(barrier, inc=1, device_id=(lax.rem(g + k, ng), t), device_id_type=MESH)
        return carry

    lax.fori_loop(1, ng, greet_group, 0)

    mine = pl.multiple_of(t * 48, 16)
    loads = [
        pltpu.make_async_copy(down, down_o, wsem.at[1]),
        pltpu.make_async_copy(qup, q_o, wsem.at[2]),
        pltpu.make_async_copy(vup, vraw, wsem.at[3]),
        pltpu.make_async_copy(w.at[:, pl.ds(0, K2)], wv.at[0], wsem.at[4]),
        pltpu.make_async_copy(w.at[:, pl.ds(K2, K2)], wv.at[1], wsem.at[5]),
    ]
    for load in loads:
        load.start()

    values = inputs[...].astype(F32)
    mean_square = jnp.mean(values * values, axis=-1, keepdims=True)
    normed = values * lax.rsqrt(mean_square + norm_eps) * gain[...].astype(F32).reshape(1, 1, 2 * K2)
    for step in range(3):
        halves = jnp.concatenate([normed[step, :, :K2], normed[step, :, K2:]], axis=0)
        X[pl.ds(pl.multiple_of(mine + step * 16, 16), 16), :] = halves.astype(BF16)
    for p in range(nt):
        pieces = [normed[step, :, p * 256 + h * 128 : p * 256 + h * 128 + 128] for h in range(2) for step in range(3)]
        xl[p * 48 : p * 48 + 48, :] = jnp.concatenate(pieces, axis=0).astype(BF16)
    lbuf[pl.ds(mine, 48), :] = xl[pl.ds(mine, 48), :]
    rsend[...] = jnp.zeros((8, 128), jnp.int32)
    rsend[0:ng, 0:PAIR_MOST] = req[...]
    spots = jnp.broadcast_to(spot_of_row[...], (nt * 8, 128)).reshape(nt, 1, 8, 128)
    tr[...] = jnp.broadcast_to(spots, (nt, 3, 8, 128)).reshape(nt * 24, 128)

    pl.semaphore_wait(barrier, nt - 1 + ng - 1)

    def piece(dx, dz, lo, n):
        rows = pl.multiple_of(dev(dx, dz) * 48, 16)
        return X.at[pl.ds(rows, 48), pl.ds(lo, n)]

    def forward(name, dx, dz, half, axis, step):
        lo, n = whole[name] if half is None else spans[name][half]
        ref = piece(dx, dz, lo, n)
        if axis == "x":
            there = dev(step, 0)
            ndx, ndz = (dx - step) % nx, dz % nz
        else:
            there = dev(0, step)
            ndx, ndz = dx % nx, (dz - step) % nz
        remote(ref, ref, gsem.at[which[name], ndx, ndz, 0 if half is None else half], g, there)

    def expect(name, dx, dz, half):
        lo, n = whole[name] if half is None else spans[name][half]
        arrived(piece(dx, dz, lo, n), gsem.at[which[name], dx % nx, dz % nz, 0 if half is None else half])

    for k in range(1, nt):
        peer = lax.rem(t + k, nt)
        remote(
            xl.at[pl.ds(pl.multiple_of(peer * 48, 16), 48), :],
            lbuf.at[pl.ds(mine, 48), :], lsem.at[nt - k], g, peer,
        )
    for k in range(1, ng):
        peer = lax.rem(g + k, ng)
        remote(rsend, rbuf.at[g], qsem.at[ng - k], peer, t)

    def lend():
        for load in loads[0:3]:
            load.wait()
        def turn(e, carry):
            column = vraw[e].astype(F32).T
            left = jnp.zeros((rank, 32), F32)
            right = jnp.zeros((rank, 64), F32)
            v_o[e] = jnp.concatenate([left, column, right], axis=-1).astype(BF16)
            return carry

        lax.fori_loop(0, own, turn, 0)
        down_f[pl.ds(g * 2, 2)] = jnp.zeros((2,) + down_f.shape[1:], BF16)
        own_spot = pl.ds(pl.multiple_of(g * 2 * rank, 16), 2 * rank)
        q_f[own_spot, :] = jnp.zeros((2 * rank, q_f.shape[1]), BF16)
        v_f[own_spot, :] = jnp.zeros((2 * rank, v_f.shape[1]), BF16)
        for k in range(1, ng):
            peer = lax.rem(g + k, ng)
            arrived(rbuf.at[peer], qsem.at[k])
            down_copy = pltpu.make_async_copy(rbuf.at[peer], rs.at[k], wsem.at[7])
            down_copy.start()
            down_copy.wait()
            for j in range(PAIR_MOST):
                slot = rs[k, g, j]
                sd[k, j] = down_o[slot]
                sq[k, j] = q_o[slot]
                sv[k, j] = v_o[slot]
            remote(sd.at[k], down_f.at[pl.ds(g * 2, 2)], fsem.at[ng - k, 0], peer, t)
            for j in range(PAIR_MOST):
                spot = pl.ds(pl.multiple_of((g * 2 + j) * rank, 16), rank)
                remote(sq.at[k, j], q_f.at[spot, :], fsem.at[ng - k, 1 + j], peer, t)
                remote(sv.at[k, j], v_f.at[spot, :], fsem.at[ng - k, 3 + j], peer, t)

    def shrink(table, first):
        def body(e, carry):
            chosen = tr[...] == e + first
            pick = jnp.concatenate([chosen, chosen], axis=-1)
            rows = jnp.where(pick, xs[...], 0.0).astype(BF16)
            part[...] += jnp.dot(rows, table[e], preferred_element_type=F32)
            return carry
        return body

    def shrink_own():
        for k in range(1, nt):
            arrived(lbuf.at[pl.ds(pl.multiple_of(lax.rem(t + k, nt) * 48, 16), 48), :], lsem.at[k])
        both = lbuf[...].astype(F32).reshape(nt, 2, 24, 128)
        xs[...] = jnp.concatenate([both[:, 0], both[:, 1]], axis=-1).reshape(nt * 24, 256)
        part[...] = jnp.zeros(part.shape, F32)
        lax.fori_loop(0, own, shrink(down_o, 0), 0)

    def shrink_far():
        for k in range(1, ng):
            peer = lax.rem(g + k, ng)
            arrived(down_f.at[pl.ds(peer * 2, 2)], fsem.at[k, 0])
        lax.fori_loop(0, ng * PAIR_MOST, shrink(down_f, own), 0)
        whole_part = part[...].reshape(nz, nx, 24, 128)
        for xx in range(nx):
            S[xx] = whole_part[:, xx].reshape(nz * 24, 128).astype(BF16)
        for k in range(1, nx):
            peer = lax.rem(x + k, nx)
            remote(S.at[peer], pbuf.at[x], p1.at[nx - k], g, z * nx + peer)

    def sum_x():
        pbuf[pl.ds(x, 1)] = S[pl.ds(x, 1)]
        for k in range(1, nx):
            arrived(pbuf.at[lax.rem(x + k, nx)], p1.at[k])
        total = pbuf[0].astype(F32)
        for xx in range(1, nx):
            total = total + pbuf[xx].astype(F32)
        blank = jnp.zeros((8, 128), F32)
        for zz in range(nz):
            half_sum[zz] = jnp.concatenate([total[zz * 24 : zz * 24 + 24], blank], axis=0).astype(BF16)
        for k in range(1, nz):
            peer = lax.rem(z + k, nz)
            remote(half_sum.at[peer], sbuf.at[z], p2.at[nz - k], g, peer * nx + x)

    def sum_z():
        sbuf[pl.ds(z, 1)] = half_sum[pl.ds(z, 1)]
        for k in range(1, nz):
            arrived(sbuf.at[lax.rem(z + k, nz)], p2.at[k])
        low = sbuf[0].astype(F32)
        for zz in range(1, nz):
            low = low + sbuf[zz].astype(F32)
        lrz[pl.ds(z, 1)] = low.astype(BF16)[None]
        for k in range(1, nz):
            peer = lax.rem(z + k, nz)
            remote(lrz.at[z], lrz.at[z], p3.at[nz - k], g, peer * nx + x)

    def spread_x():
        for k in range(1, nz):
            arrived(lrz.at[lax.rem(z + k, nz)], p3.at[k])
        lrall[pl.ds(x, 1)] = lrz[...][None]
        for k in range(1, nx):
            peer = lax.rem(x + k, nx)
            remote(lrz, lrall.at[x], p4.at[nx - k], g, z * nx + peer)

    def expand():
        for k in range(1, nx):
            arrived(lrall.at[lax.rem(x + k, nx)], p4.at[k])
        for k in range(1, ng):
            peer = lax.rem(g + k, ng)
            for j in range(PAIR_MOST):
                spot = pl.ds(pl.multiple_of((peer * 2 + j) * rank, 16), rank)
                arrived(q_f.at[spot, :], fsem.at[k, 1 + j])
                arrived(v_f.at[spot, :], fsem.at[k, 3 + j])

        for zz in range(nz):
            for xx in range(nx):
                low24 = lrall[xx, zz].astype(F32)[:24]
                spot = pl.ds((zz * nx + xx) * 24, 24)
                LRq[spot, :] = jnp.concatenate([low24[:, :64], low24[:, :64]], axis=-1)
                LRv[spot, :] = jnp.concatenate([low24[:, 64:], low24[:, 64:]], axis=-1)
        Dq[...] = jnp.zeros(Dq.shape, F32)
        Dv[...] = jnp.zeros(Dv.shape, F32)

        def grow(q_table, v_table, first):
            def body(i, carry):
                lane = lax.broadcasted_iota(jnp.int32, (nt * 24, 128), 1) // 64
                hit0 = tr[...] == lane + (i * 4 + first)
                hit1 = tr[...] == lane + (i * 4 + 2 + first)
                spread_q = jnp.concatenate([jnp.where(hit0, LRq[...], 0.0), jnp.where(hit1, LRq[...], 0.0)], axis=-1)
                spread_v = jnp.concatenate([jnp.where(hit0, LRv[...], 0.0), jnp.where(hit1, LRv[...], 0.0)], axis=-1)
                Dq[...] += jnp.dot(spread_q.astype(BF16), q_table(i), preferred_element_type=F32)
                Dv[...] += jnp.dot(spread_v.astype(BF16), v_table(i), preferred_element_type=F32)
                return carry
            return body

        def own_table(ref):
            return lambda i: ref[pl.ds(i * 4, 4)].reshape(4 * rank, ref.shape[2])

        def far_table(ref):
            return lambda i: ref[pl.ds(pl.multiple_of(i * 4 * rank, 4 * rank), 4 * rank), :]

        lax.fori_loop(0, own // 4, grow(own_table(q_o), own_table(v_o), 0), 0)
        lax.fori_loop(0, ng * PAIR_MOST // 4, grow(far_table(q_f), far_table(v_f), own), 0)

    kt = 512

    def base_of(dz):
        rows = pl.ds(pl.multiple_of(lax.rem(z + dz % nz, nz) * (nx * 48), 16), nx * 48)
        acc[...] = jnp.zeros(acc.shape, F32)

        def body(k, carry):
            cols = pl.ds(pl.multiple_of(k * kt, kt), kt)
            for h in range(2):
                acc[h] += lax.dot_general(
                    X[rows, cols], wv[h, :, cols], (((1,), (1,)), ((), ())), preferred_element_type=F32
                )
            return carry

        lax.fori_loop(0, K2 // kt, body, 0)
        first = acc[0].reshape(nx * 3, 2, 8, NW)[:, 0]
        second = acc[1].reshape(nx * 3, 2, 8, NW)[:, 1]
        plain[dz % nz] = (first + second).reshape(nx * 24, NW)

    def finish(dz):
        base = plain[dz % nz]
        zz = lax.rem(z + dz % nz, nz)
        rows = pl.ds(pl.multiple_of(zz * (nx * 24), 8), nx * 24)
        query = base[:, :256] + adapter_scale * Dq[rows, :]
        keyval = base[:, 256:320] + adapter_scale * Dv[rows, :][:, :64]
        for xx in range(nx):
            q = query[xx * 24 : xx * 24 + 24]
            kv = keyval[xx * 24 : xx * 24 + 24]
            block = jnp.concatenate(
                [
                    q[:, :128], q[:, 128:],
                    jnp.concatenate([kv[0:8], kv[8:16]], axis=-1),
                    jnp.concatenate([kv[16:24], jnp.zeros((8, 64), F32)], axis=-1),
                ],
                axis=0,
            )
            ob[dz % nz, xx] = block.astype(BF16)
        for dx in range(nx):
            xx = lax.rem(x + dx, nx)
            if dx == 0 and dz % nz == 0:
                keep = pltpu.make_async_copy(ob.at[0, xx], out.at[t], wsem.at[8])
                keep.start()
                keep.wait()
            else:
                remote(ob.at[dz % nz, xx], out.at[t], osem.at[(-dx) % nx, (-dz) % nz], g, zz * nx + xx)

    chores = [
        (CHORES[0], lend), (CHORES[1], shrink_own), (CHORES[2], shrink_far), (CHORES[3], sum_x),
        (CHORES[4], sum_z), (CHORES[5], spread_x), (CHORES[6], expand),
    ]
    loaded = []
    ready = []
    based = []
    missing = {dz: 2 * nx for dz in range(nz)}
    missing[0] -= 2

    def settle(now):
        while chores and chores[0][0] <= now:
            chores.pop(0)[1]()
        while ready:
            if not loaded:
                for load in loads[3:5]:
                    load.wait()
                loaded.append(1)
            dz = ready.pop(0)
            base_of(dz)
            based.append(dz)
        while based and not chores:
            finish(based.pop(0))

    for kind, when, name, dx, dz, half in ring_order(nx, nz, LA, LB):
        if kind == "send":
            axis, step = when
            forward(name, dx, dz, half, axis, step)
        else:
            settle(when)
            piece_half, last = (None, True) if half is None else half
            expect(name, dx, dz, piece_half)
            if last:
                missing[dz] -= 1
                if missing[dz] == 0:
                    ready.append(dz)
    settle(1e9)

    for dz in range(nz):
        for dx in range(nx):
            if dx or dz:
                arrived(out.at[dev(dx, dz)], osem.at[dx, dz])
    for copy in pending:
        copy.wait_send()


def project(nx, nz, ng, inputs, gain, w, down, qup, vup, req, spot_of_row):
    nt = nx * nz
    K2 = inputs.shape[2] // 2
    own = down.shape[0]
    NW = w.shape[0]
    DMA = pltpu.SemaphoreType.DMA
    vmem = pl.BlockSpec(memory_space=pltpu.VMEM)
    hbm = pl.BlockSpec(memory_space=pl.ANY)
    sends = (nt - 1) + (ng - 1) * 6 + 5 * nt + 2 * (nx + nz) + 64 + nt + 160
    rows = nt * 24
    return pl.pallas_call(
        functools.partial(project_kernel, nx, nz, ng, own),
        out_shape=jax.ShapeDtypeStruct((nt, 64, 128), BF16),
        in_specs=[vmem, vmem, hbm, hbm, hbm, hbm, vmem, vmem],
        out_specs=vmem,
        scratch_shapes=[
            pltpu.VMEM((nt * 48, K2), BF16),
            pltpu.VMEM((nt * 48, 128), BF16),
            pltpu.VMEM((rows, 128), jnp.int32),
            pltpu.VMEM((2, NW, K2), BF16),
            pltpu.VMEM(vup.shape, BF16),
            pltpu.VMEM((nt * 48, 128), BF16),
            pltpu.VMEM((rows, 256), F32),
            pltpu.VMEM(down.shape, BF16),
            pltpu.VMEM(qup.shape, BF16),
            pltpu.VMEM((own, 64, 128), BF16),
            pltpu.VMEM((ng * 2,) + down.shape[1:], BF16),
            pltpu.VMEM((ng * 2 * 64, 256), BF16),
            pltpu.VMEM((ng * 2 * 64, 128), BF16),
            pltpu.VMEM((ng, 2) + down.shape[1:], BF16),
            pltpu.VMEM((ng, 2, 64, 256), BF16),
            pltpu.VMEM((ng, 2, 64, 128), BF16),
            pltpu.VMEM((ng, 8, 128), jnp.int32),
            pltpu.VMEM((8, 128), jnp.int32),
            pltpu.SMEM((ng, 8, 128), jnp.int32),
            pltpu.VMEM((rows, 128), F32),
            pltpu.VMEM((nx, nz * 24, 128), BF16),
            pltpu.VMEM((nx, nz * 24, 128), BF16),
            pltpu.VMEM((nz, 32, 128), BF16),
            pltpu.VMEM((nz, 32, 128), BF16),
            pltpu.VMEM((nz, 32, 128), BF16),
            pltpu.VMEM((nx, nz, 32, 128), BF16),
            pltpu.VMEM((rows, 128), F32),
            pltpu.VMEM((rows, 128), F32),
            pltpu.VMEM((rows, 256), F32),
            pltpu.VMEM((rows, 128), F32),
            pltpu.VMEM((2, nx * 48, NW), F32),
            pltpu.VMEM((nz, nx * 24, NW), F32),
            pltpu.VMEM((nz, nx, 64, 128), BF16),
            DMA((sends,)),
            DMA((2, nx, nz, 2)),
            DMA((nt,)),
            DMA((1,)),
            DMA((ng, 5)),
            DMA((ng,)),
            DMA((nx,)),
            DMA((nz,)),
            DMA((nz,)),
            DMA((nx,)),
            DMA((nx, nz)),
            DMA((9,)),
        ],
        compiler_params=pltpu.CompilerParams(
            collective_id=0, has_side_effects=True, vmem_limit_bytes=56 * MIB
        ),
        name="project",
    )(inputs, gain, w, down, qup, vup, req, spot_of_row)


def attend_kernel(lengths, got, cos, sin, keys, values, out, scr, res):
    rows_here, window, _ = keys.shape
    factor = HEAD_DIM ** (-0.5)
    dims = (((1,), (1,)), ((), ()))
    lane = lax.broadcasted_iota(jnp.int32, (8, 128), 1) // 32

    def turned(v, c, n):
        return v * c + pltpu.roll(v, 64, 1) * n

    for b in range(8):
        block = got[b].astype(F32)
        for hh in range(2):
            scr[b, hh * 24 : hh * 24 + 24, :] = turned(block[hh * 24 : hh * 24 + 24], cos[...], sin[...])
        scr[b, 48:64, :] = block[48:64]

    def gathered(head, row, offset):
        total = jnp.zeros((8, 128), F32)
        for b in range(4):
            moved = pltpu.roll(scr[4 * head + b, row : row + 8, :], (32 * b - offset) % 128, 1)
            total = jnp.where(lane == b, moved, total)
        return total

    pad = jnp.zeros((8, 128), F32)
    fresh_keys = []
    fresh_values = []
    for e in range(2):
        new = [gathered(e, 48, 0), gathered(e, 48, 64), gathered(e, 56, 0)]
        new = turned(jnp.concatenate(new, axis=0), cos[...], sin[...])
        fresh_keys.append(jnp.concatenate([new, pad], axis=0))
        new = [gathered(e, 48, 32), gathered(e, 48, 96), gathered(e, 56, 32), pad]
        fresh_values.append(jnp.concatenate(new, axis=0))
    fresh_keys = jnp.concatenate(fresh_keys, axis=-1).astype(BF16)
    fresh_values = jnp.concatenate(fresh_values, axis=-1).astype(BF16)

    blank = jnp.zeros((32, 128), F32)
    column = lax.broadcasted_iota(jnp.int32, (64, window), 1)
    queries = []
    past = []
    for r in range(rows_here):
        q = [
            jnp.concatenate([scr[4 * e + b, pl.ds(r, 8, stride=8), :] for b in range(4)], axis=0)
            for e in range(2)
        ]
        q = jnp.concatenate(
            [jnp.concatenate([q[0], blank], axis=-1), jnp.concatenate([blank, q[1]], axis=-1)], axis=0
        ).astype(BF16)
        queries.append(q)
        score = lax.dot_general(q, keys[r], dims, preferred_element_type=F32) * factor
        past.append(jnp.where(column < lengths[r], score, -jnp.inf))
    queries = jnp.concatenate(queries, axis=0)
    past = jnp.concatenate(past, axis=0)
    fresh = lax.dot_general(queries, fresh_keys, dims, preferred_element_type=F32) * factor
    at = lax.broadcasted_iota(jnp.int32, fresh.shape, 0)
    fresh_at = lax.broadcasted_iota(jnp.int32, fresh.shape, 1)
    order = at % 8
    step = jnp.where(order >= 3, order - 3, order)
    own_row = at // 64 == fresh_at % 8
    fresh_live = jnp.logical_and(own_row, jnp.logical_and(fresh_at // 8 <= step, fresh_at < 24))
    fresh = jnp.where(fresh_live, fresh, -jnp.inf)
    highest = jnp.maximum(
        jnp.max(past, axis=-1, keepdims=True), jnp.max(fresh, axis=-1, keepdims=True)
    )
    past = jnp.exp(past - highest)
    fresh = jnp.exp(fresh - highest)
    total = jnp.sum(past, axis=-1, keepdims=True) + jnp.sum(fresh, axis=-1, keepdims=True)
    past = (past / total).astype(BF16)
    fresh = (fresh / total).astype(BF16)
    context = jnp.dot(fresh, fresh_values, preferred_element_type=F32)
    for r in range(rows_here):
        rows = slice(r * 64, (r + 1) * 64)
        part = context[rows] + jnp.dot(past[rows], values[r], preferred_element_type=F32)
        for e in range(2):
            for b in range(4):
                res[4 * e + b, r * 8 : r * 8 + 8, :] = part[
                    32 * e + b * 8 : 32 * e + b * 8 + 8, 128 * e : 128 * e + 128
                ]
    for b in range(8):
        for hh in range(2):
            for k in range(3):
                spot = slice((2 * b + hh) * 128, (2 * b + hh) * 128 + 128)
                out[k, :, spot] = res[b, pl.ds(hh * 3 + k, 8, stride=8), :].astype(BF16)


def attend(lengths, got, cos, sin, hist):
    rows, window, width = hist.shape
    steps = cos.shape[0] // rows
    pairs = got.shape[0] // 8
    return pl.pallas_call(
        attend_kernel,
        out_shape=jax.ShapeDtypeStruct((steps, rows, HEADS * HEAD_DIM), BF16),
        grid=(pairs,),
        in_specs=[
            pl.BlockSpec(memory_space=pltpu.SMEM),
            pl.BlockSpec((8, 64, 128), lambda h: (h, 0, 0)),
            pl.BlockSpec((steps * rows, 128), lambda h: (0, 0)),
            pl.BlockSpec((steps * rows, 128), lambda h: (0, 0)),
            pl.BlockSpec((rows, window, 2 * HEAD_DIM), lambda h: (0, 0, h)),
            pl.BlockSpec((rows, window, 2 * HEAD_DIM), lambda h: (0, 0, KV_HEADS // 2 + h)),
        ],
        out_specs=pl.BlockSpec((steps, rows, 2 * HEADS // KV_HEADS * HEAD_DIM), lambda h: (0, 0, h)),
        scratch_shapes=[pltpu.VMEM((8, 64, 128), F32), pltpu.VMEM((8, 64, 128), F32)],
        compiler_params=pltpu.CompilerParams(vmem_limit_bytes=56 * MIB),
        name="attend",
    )(lengths, got, cos, sin, hist, hist)


def routing(adapter_slot, row_adapter, store, groups, home):
    slots = adapter_slot.shape[0]
    catalog = jnp.arange(slots, dtype=jnp.int32)
    by_adapter = row_adapter[:, None] == catalog[None, :]
    slot_of_row = jnp.sum(jnp.where(by_adapter, adapter_slot[None, :], 0), axis=1)
    by_slot = slot_of_row[:, None] == catalog[None, :]
    source = slot_of_row // store
    offset = slot_of_row % store
    wanted = jnp.any(by_slot, axis=0).reshape(groups, store)
    foreign = jnp.logical_and(wanted, jnp.arange(groups, dtype=jnp.int32)[:, None] != home)
    marked = foreign.astype(jnp.int32)
    ranking = jnp.cumsum(marked, axis=1) - marked
    chosen = jnp.logical_and(
        foreign[:, :, None],
        ranking[:, :, None] == jnp.arange(PAIR_MOST, dtype=jnp.int32)[None, None, :],
    )
    request = jnp.sum(
        jnp.where(chosen, jnp.arange(store, dtype=jnp.int32)[None, :, None], 0), axis=1
    )
    row_rank = jnp.sum(jnp.where(by_slot, ranking.reshape(-1)[None, :], 0), axis=1)
    table_row = jnp.where(source == home, offset, store + source * PAIR_MOST + row_rank)
    return request, table_row


def projected(
    inputs, norm_gain, united_weight, adapter_down, query_up, value_up, adapter_slot, row_adapter
):
    steps, rows_here, width = inputs.shape
    nt = lax.axis_size("tensor")
    ng = lax.axis_size("group")
    nx = NX
    nz = nt // nx
    g = lax.axis_index("group")
    request, table_row = routing(adapter_slot, row_adapter, adapter_down.shape[0], ng, g)
    return project(
        nx, nz, ng, inputs, norm_gain, united_weight.T, adapter_down, query_up,
        value_up.transpose(0, 2, 1), request, table_row[:, None],
    )


def local(
    inputs, norm_gain, united_weight, adapter_down, query_up, value_up, history,
    adapter_slot, row_adapter, cache_length,
):
    steps, rows_here, width = inputs.shape
    nt = lax.axis_size("tensor")
    t = lax.axis_index("tensor")
    got = projected(
        inputs, norm_gain, united_weight, adapter_down, query_up, value_up, adapter_slot, row_adapter
    )
    lengths = lax.dynamic_slice_in_dim(cache_length, t * rows_here, rows_here, 0)
    positions = lengths[None, :] + jnp.arange(steps, dtype=jnp.int32)[:, None]
    cos, sin = rope_tables(positions.reshape(-1))
    return attend(lengths, got, cos, sin, history)


def solution(mesh):
    in_specs = (
        P(None, ("group", "tensor"), None),
        P(),
        P(None, "tensor"),
        P("group", "tensor", None),
        P("group", None, "tensor"),
        P("group", None, "tensor"),
        P(("group", "tensor"), None, None),
        P(),
        P("group"),
        P("group"),
    )
    out_specs = P(None, ("group", "tensor"), None)
    return jax.shard_map(local, mesh=mesh, in_specs=in_specs, out_specs=out_specs, check_vma=False)
```

```python
import functools
import heapq
import math

import jax
import jax.numpy as jnp
from jax import lax
from jax.experimental import pallas as pl
from jax.experimental.pallas import tpu as pltpu
from jax.sharding import PartitionSpec as P

HEADS = 64
KV_HEADS = 8
HEAD_DIM = 128
PAIR_MOST = 2
NX = 4

adapter_scale = 0.5
rope_base = 500000.0
norm_eps = 1e-05
MIB = 1024 * 1024
F32 = jnp.float32
BF16 = jnp.bfloat16
MESH = pl.DeviceIdType.MESH


CHORES = (3.0, 16.0, 30.0, 41.0, 50.0, 58.0, 66.0)
BUSY = {"x": 4.0, "z": 8.0}
RATE = 39e3
LOOK = 6.0
RANKED = False


def ring_order(nx, nz, la, lb):
    sizes = {"A": la * 96 / RATE, "B": lb * 96 / RATE}
    span = {"x": nx, "z": nz}
    links = [("x", 1), ("x", -1), ("z", 1), ("z", -1)]
    free = {key: BUSY[key[0]] for key in links}
    waiting = {key: [] for key in links}
    asleep = {key: True for key in links}
    heap = []
    halves = {}
    out = []
    count = [0]

    def push(when, what):
        count[0] += 1
        heapq.heappush(heap, (when, count[0], what))

    def send(now, name, dx, dz, half, axis, step, rank):
        key = (axis, step)
        count[0] += 1
        heapq.heappush(waiting[key], (rank, count[0], name, dx % nx, dz % nz, half))
        if asleep[key]:
            asleep[key] = False
            push(max(now, free[key] - LOOK), ("pick", key))

    def rank_of(name, axis, hop):
        if name == "B" and axis == "z":
            return 0
        if name == "A" and axis == "x":
            return 0
        return 5 - hop if RANKED else 1

    def launch(now, name, dx, dz, axis):
        if span[axis] > 2:
            for step in (1, -1):
                send(now, name, dx, dz, None, axis, step, rank_of(name, axis, 0))
        elif span[axis] == 2:
            send(now, name, dx, dz, 0, axis, 1, rank_of(name, axis, 0))
            send(now, name, dx, dz, 1, axis, -1, rank_of(name, axis, 0))

    launch(0.0, "A", 0, 0, "x")
    launch(0.0, "B", 0, 0, "z")
    launch(0.0, "B", 0, 0, "x")
    launch(0.0, "A", 0, 0, "z")
    while heap:
        now, _, what = heapq.heappop(heap)
        if what[0] == "pick":
            key = what[1]
            if not waiting[key]:
                asleep[key] = True
                continue
            _, _, name, dx, dz, half = heapq.heappop(waiting[key])
            axis, step = key
            free[key] = max(free[key], now) + sizes[name] * (1.0 if half is None else 0.5)
            out.append(("send", key, name, dx, dz, half))
            ndx = (dx - (step if axis == "x" else 0)) % nx
            ndz = (dz - (step if axis == "z" else 0)) % nz
            push(free[key] + 1.5, ("land", name, ndx, ndz, half, axis, step))
            push(max(now, free[key] - LOOK), ("pick", key))
            continue
        _, name, dx, dz, half, axis, step = what
        tie = (name, dx, dz)
        seen = halves.get(tie, 0)
        halves[tie] = seen + 1
        last = half is None or seen == 1
        out.append(("wait", now, name, dx, dz, half if half is None else (half, last)))
        size = span[axis]
        far = (-step * (dx if axis == "x" else dz)) % size
        if half is None:
            if far + 1 < size // 2:
                send(now, name, dx, dz, None, axis, step, rank_of(name, axis, far))
            elif far + 1 == size // 2:
                send(now, name, dx, dz, 0 if step > 0 else 1, axis, step, rank_of(name, axis, far))
        if last:
            if name == "A" and axis == "x":
                launch(now, name, dx, dz, "z")
            if name == "B" and axis == "z":
                launch(now, name, dx, dz, "x")
    return out


def project_kernel(
    nx, nz, ng, own,
    inputs, gain, w, down, qup, vup, spots_and_slots,
    out,
    X, xl, tr, wv, vraw, lbuf, xs, down_o, q_o, v_o, down_f, q_f, v_f, sd, sq, sv, rbuf, rsend, rs,
    part, pbuf, S, half_sum, sbuf, lrz, lrall, LRq, LRv, Dq, Dv, plain, ob,
    ssem, gsem, lsem, dsem, fsem, qsem, p1, p2, p3, p4, osem, wsem,
):
    nt = nx * nz
    K2 = X.shape[1]
    NW = w.shape[0]
    rank = 64
    tiles = K2 // 128
    ta = max((tiles * 12) // 32, 2)
    LA = ta * 128
    LB = K2 - LA
    spans = {
        "A": ((0, (ta // 2) * 128), ((ta // 2) * 128, LA - (ta // 2) * 128)),
        "B": ((LA, ((tiles - ta) // 2) * 128), (LA + ((tiles - ta) // 2) * 128, LB - ((tiles - ta) // 2) * 128)),
    }
    whole = {"A": (0, LA), "B": (LA, LB)}
    which = {"A": 0, "B": 1}

    g = lax.axis_index("group")
    t = lax.axis_index("tensor")
    z = t // nx
    x = t % nx

    def dev(dx, dz):
        return lax.rem(z + (dz % nz), nz) * nx + lax.rem(x + (dx % nx), nx)

    pending = []
    counter = [0]

    def remote(src, dst, rsem, group, tensor):
        sem = ssem.at[counter[0]]
        counter[0] += 1
        copy = pltpu.make_async_remote_copy(
            src_ref=src, dst_ref=dst, send_sem=sem, recv_sem=rsem,
            device_id=(group, tensor), device_id_type=MESH,
        )
        copy.start()
        pending.append(copy)

    def arrived(ref, sem):
        pltpu.make_async_copy(ref, ref, sem).wait()

    barrier = pltpu.get_barrier_semaphore()

    def greet(k, carry):
        pl.semaphore_signal(barrier, inc=1, device_id=(g, lax.rem(t + k, nt)), device_id_type=MESH)
        return carry

    lax.fori_loop(1, nt, greet, 0)

    def greet_group(k, carry):
        pl.semaphore_signal(barrier, inc=1, device_id=(lax.rem(g + k, ng), t), device_id_type=MESH)
        return carry

    lax.fori_loop(1, ng, greet_group, 0)

    mine = pl.multiple_of(t * 48, 16)
    loads = [
        pltpu.make_async_copy(down, down_o, wsem.at[1]),
        pltpu.make_async_copy(qup, q_o, wsem.at[2]),
        pltpu.make_async_copy(vup, vraw, wsem.at[3]),
        pltpu.make_async_copy(w.at[:, pl.ds(0, K2)], wv.at[0], wsem.at[4]),
        pltpu.make_async_copy(w.at[:, pl.ds(K2, K2)], wv.at[1], wsem.at[5]),
    ]
    for load in loads:
        load.start()

    values = inputs[...].astype(F32)
    mean_square = jnp.mean(values * values, axis=-1, keepdims=True)
    normed = values * lax.rsqrt(mean_square + norm_eps) * gain[...].astype(F32).reshape(1, 1, 2 * K2)
    for step in range(3):
        halves = jnp.concatenate([normed[step, :, :K2], normed[step, :, K2:]], axis=0)
        X[pl.ds(pl.multiple_of(mine + step * 16, 16), 16), :] = halves.astype(BF16)
    for p in range(nt):
        pieces = [normed[step, :, p * 256 + h * 128 : p * 256 + h * 128 + 128] for h in range(2) for step in range(3)]
        xl[p * 48 : p * 48 + 48, :] = jnp.concatenate(pieces, axis=0).astype(BF16)
    lbuf[pl.ds(mine, 48), :] = xl[pl.ds(mine, 48), :]
    rsend[...] = jnp.broadcast_to(spots_and_slots[nt * 8 : nt * 8 + 16, :], (16, 128))
    spots = jnp.broadcast_to(spots_and_slots[0 : nt * 8, :], (nt * 8, 128)).reshape(nt, 1, 8, 128)
    tr[...] = jnp.broadcast_to(spots, (nt, 3, 8, 128)).reshape(nt * 24, 128)

    pl.semaphore_wait(barrier, nt - 1 + ng - 1)

    def piece(dx, dz, lo, n):
        rows = pl.multiple_of(dev(dx, dz) * 48, 16)
        return X.at[pl.ds(rows, 48), pl.ds(lo, n)]

    def forward(name, dx, dz, half, axis, step):
        lo, n = whole[name] if half is None else spans[name][half]
        ref = piece(dx, dz, lo, n)
        if axis == "x":
            there = dev(step, 0)
            ndx, ndz = (dx - step) % nx, dz % nz
        else:
            there = dev(0, step)
            ndx, ndz = dx % nx, (dz - step) % nz
        remote(ref, ref, gsem.at[which[name], ndx, ndz, 0 if half is None else half], g, there)

    def expect(name, dx, dz, half):
        lo, n = whole[name] if half is None else spans[name][half]
        arrived(piece(dx, dz, lo, n), gsem.at[which[name], dx % nx, dz % nz, 0 if half is None else half])

    for k in range(1, nt):
        peer = lax.rem(t + k, nt)
        remote(
            xl.at[pl.ds(pl.multiple_of(peer * 48, 16), 48), :],
            lbuf.at[pl.ds(mine, 48), :], lsem.at[nt - k], g, peer,
        )
    for k in range(1, ng):
        peer = lax.rem(g + k, ng)
        remote(rsend, rbuf.at[g], qsem.at[ng - k], peer, t)

    def lend():
        for load in loads[0:3]:
            load.wait()
        def turn(e, carry):
            column = vraw[e].astype(F32).T
            left = jnp.zeros((rank, 32), F32)
            right = jnp.zeros((rank, 64), F32)
            v_o[e] = jnp.concatenate([left, column, right], axis=-1).astype(BF16)
            return carry

        lax.fori_loop(0, own, turn, 0)
        down_f[pl.ds(g * 2, 2)] = jnp.zeros((2,) + down_f.shape[1:], BF16)
        own_spot = pl.ds(pl.multiple_of(g * 2 * rank, 16), 2 * rank)
        q_f[own_spot, :] = jnp.zeros((2 * rank, q_f.shape[1]), BF16)
        v_f[own_spot, :] = jnp.zeros((2 * rank, v_f.shape[1]), BF16)
        for k in range(1, ng):
            peer = lax.rem(g + k, ng)
            arrived(rbuf.at[peer], qsem.at[k])
            down_copy = pltpu.make_async_copy(rbuf.at[peer], rs.at[k], wsem.at[7])
            down_copy.start()
            down_copy.wait()
            for j in range(PAIR_MOST):
                slot = rs[k, PAIR_MOST * g + j, 0]
                sd[k, j] = down_o[slot]
                sq[k, j] = q_o[slot]
                sv[k, j] = v_o[slot]
            remote(sd.at[k], down_f.at[pl.ds(g * 2, 2)], fsem.at[ng - k, 0], peer, t)
            for j in range(PAIR_MOST):
                spot = pl.ds(pl.multiple_of((g * 2 + j) * rank, 16), rank)
                remote(sq.at[k, j], q_f.at[spot, :], fsem.at[ng - k, 1 + j], peer, t)
                remote(sv.at[k, j], v_f.at[spot, :], fsem.at[ng - k, 3 + j], peer, t)

    def shrink(table, first):
        def body(e, carry):
            chosen = tr[...] == e + first
            pick = jnp.concatenate([chosen, chosen], axis=-1)
            rows = jnp.where(pick, xs[...], 0.0).astype(BF16)
            part[...] += jnp.dot(rows, table[e], preferred_element_type=F32)
            return carry
        return body

    def shrink_own():
        for k in range(1, nt):
            arrived(lbuf.at[pl.ds(pl.multiple_of(lax.rem(t + k, nt) * 48, 16), 48), :], lsem.at[k])
        both = lbuf[...].astype(F32).reshape(nt, 2, 24, 128)
        xs[...] = jnp.concatenate([both[:, 0], both[:, 1]], axis=-1).reshape(nt * 24, 256)
        part[...] = jnp.zeros(part.shape, F32)
        lax.fori_loop(0, own, shrink(down_o, 0), 0)

    def shrink_far():
        for k in range(1, ng):
            peer = lax.rem(g + k, ng)
            arrived(down_f.at[pl.ds(peer * 2, 2)], fsem.at[k, 0])
        lax.fori_loop(0, ng * PAIR_MOST, shrink(down_f, own), 0)
        whole_part = part[...].reshape(nz, nx, 24, 128)
        for xx in range(nx):
            S[xx] = whole_part[:, xx].reshape(nz * 24, 128).astype(BF16)
        for k in range(1, nx):
            peer = lax.rem(x + k, nx)
            remote(S.at[peer], pbuf.at[x], p1.at[nx - k], g, z * nx + peer)

    def sum_x():
        pbuf[pl.ds(x, 1)] = S[pl.ds(x, 1)]
        for k in range(1, nx):
            arrived(pbuf.at[lax.rem(x + k, nx)], p1.at[k])
        total = pbuf[0].astype(F32)
        for xx in range(1, nx):
            total = total + pbuf[xx].astype(F32)
        blank = jnp.zeros((8, 128), F32)
        for zz in range(nz):
            half_sum[zz] = jnp.concatenate([total[zz * 24 : zz * 24 + 24], blank], axis=0).astype(BF16)
        for k in range(1, nz):
            peer = lax.rem(z + k, nz)
            remote(half_sum.at[peer], sbuf.at[z], p2.at[nz - k], g, peer * nx + x)

    def sum_z():
        sbuf[pl.ds(z, 1)] = half_sum[pl.ds(z, 1)]
        for k in range(1, nz):
            arrived(sbuf.at[lax.rem(z + k, nz)], p2.at[k])
        low = sbuf[0].astype(F32)
        for zz in range(1, nz):
            low = low + sbuf[zz].astype(F32)
        lrz[pl.ds(z, 1)] = low.astype(BF16)[None]
        for k in range(1, nz):
            peer = lax.rem(z + k, nz)
            remote(lrz.at[z], lrz.at[z], p3.at[nz - k], g, peer * nx + x)

    def spread_x():
        for k in range(1, nz):
            arrived(lrz.at[lax.rem(z + k, nz)], p3.at[k])
        lrall[pl.ds(x, 1)] = lrz[...][None]
        for k in range(1, nx):
            peer = lax.rem(x + k, nx)
            remote(lrz, lrall.at[x], p4.at[nx - k], g, z * nx + peer)

    def expand():
        for k in range(1, nx):
            arrived(lrall.at[lax.rem(x + k, nx)], p4.at[k])
        for k in range(1, ng):
            peer = lax.rem(g + k, ng)
            for j in range(PAIR_MOST):
                spot = pl.ds(pl.multiple_of((peer * 2 + j) * rank, 16), rank)
                arrived(q_f.at[spot, :], fsem.at[k, 1 + j])
                arrived(v_f.at[spot, :], fsem.at[k, 3 + j])

        for zz in range(nz):
            for xx in range(nx):
                low24 = lrall[xx, zz].astype(F32)[:24]
                spot = pl.ds((zz * nx + xx) * 24, 24)
                LRq[spot, :] = jnp.concatenate([low24[:, :64], low24[:, :64]], axis=-1)
                LRv[spot, :] = jnp.concatenate([low24[:, 64:], low24[:, 64:]], axis=-1)
        Dq[...] = jnp.zeros(Dq.shape, F32)
        Dv[...] = jnp.zeros(Dv.shape, F32)

        def grow(q_table, v_table, first):
            def body(i, carry):
                lane = lax.broadcasted_iota(jnp.int32, (nt * 24, 128), 1) // 64
                hit0 = tr[...] == lane + (i * 4 + first)
                hit1 = tr[...] == lane + (i * 4 + 2 + first)
                spread_q = jnp.concatenate([jnp.where(hit0, LRq[...], 0.0), jnp.where(hit1, LRq[...], 0.0)], axis=-1)
                spread_v = jnp.concatenate([jnp.where(hit0, LRv[...], 0.0), jnp.where(hit1, LRv[...], 0.0)], axis=-1)
                Dq[...] += jnp.dot(spread_q.astype(BF16), q_table(i), preferred_element_type=F32)
                Dv[...] += jnp.dot(spread_v.astype(BF16), v_table(i), preferred_element_type=F32)
                return carry
            return body

        def own_table(ref):
            return lambda i: ref[pl.ds(i * 4, 4)].reshape(4 * rank, ref.shape[2])

        def far_table(ref):
            return lambda i: ref[pl.ds(pl.multiple_of(i * 4 * rank, 4 * rank), 4 * rank), :]

        lax.fori_loop(0, own // 4, grow(own_table(q_o), own_table(v_o), 0), 0)
        lax.fori_loop(0, ng * PAIR_MOST // 4, grow(far_table(q_f), far_table(v_f), own), 0)

    kt = 128 * math.gcd(ta, tiles, 4)
    seen = {dz: [] for dz in range(nz)}

    def multiply(dz, name):
        rows = pl.ds(pl.multiple_of(lax.rem(z + dz % nz, nz) * (nx * 48), 16), nx * 48)
        lo, n = whole[name]

        def body(k, carry):
            cols = pl.ds(pl.multiple_of(lo + k * kt, kt), kt)
            for h in range(2):
                plain[dz, h] += lax.dot_general(
                    wv[h, :, cols], X[rows, cols], (((1,), (1,)), ((), ())), preferred_element_type=F32
                )
            return carry

        if name not in seen[dz] and not seen[dz]:
            plain[dz] = jnp.zeros(plain.shape[1:], F32)
        seen[dz].append(name)
        lax.fori_loop(0, n // kt, body, 0)

    def base_of(dz):
        first = plain[dz, 0].T.reshape(nx * 3, 2, 8, NW)[:, 0]
        second = plain[dz, 1].T.reshape(nx * 3, 2, 8, NW)[:, 1]
        return (first + second).reshape(nx * 24, NW)

    def finish(dz):
        base = base_of(dz % nz)
        zz = lax.rem(z + dz % nz, nz)
        rows = pl.ds(pl.multiple_of(zz * (nx * 24), 8), nx * 24)
        query = base[:, :256] + adapter_scale * Dq[rows, :]
        keyval = base[:, 256:320] + adapter_scale * Dv[rows, :][:, :64]
        for xx in range(nx):
            q = query[xx * 24 : xx * 24 + 24]
            kv = keyval[xx * 24 : xx * 24 + 24]
            block = jnp.concatenate(
                [
                    q[:, :128], q[:, 128:],
                    jnp.concatenate([kv[0:8], kv[8:16]], axis=-1),
                    jnp.concatenate([kv[16:24], jnp.zeros((8, 64), F32)], axis=-1),
                ],
                axis=0,
            )
            ob[dz % nz, xx] = block.astype(BF16)
        for dx in range(nx):
            xx = lax.rem(x + dx, nx)
            if dx == 0 and dz % nz == 0:
                keep = pltpu.make_async_copy(ob.at[0, xx], out.at[t], wsem.at[8])
                keep.start()
                keep.wait()
            else:
                remote(ob.at[dz % nz, xx], out.at[t], osem.at[(-dx) % nx, (-dz) % nz], g, zz * nx + xx)

    chores = [
        (CHORES[0], lend), (CHORES[1], shrink_own), (CHORES[2], shrink_far), (CHORES[3], sum_x),
        (CHORES[4], sum_z), (CHORES[5], spread_x), (CHORES[6], expand),
    ]
    loaded = []
    ready = []
    based = []
    missing = {(dz, name): nx - (dz == 0) for dz in range(nz) for name in "AB"}

    def settle(now):
        while chores and chores[0][0] <= now:
            chores.pop(0)[1]()
        while ready:
            if not loaded:
                for load in loads[3:5]:
                    load.wait()
                loaded.append(1)
            dz, name = ready.pop(0)
            multiply(dz, name)
            if len(seen[dz]) == 2:
                based.append(dz)
        while based and not chores:
            finish(based.pop(0))

    for kind, when, name, dx, dz, half in ring_order(nx, nz, LA, LB):
        if kind == "send":
            axis, step = when
            forward(name, dx, dz, half, axis, step)
        else:
            settle(when)
            piece_half, last = (None, True) if half is None else half
            expect(name, dx, dz, piece_half)
            if last:
                missing[dz, name] -= 1
                if missing[dz, name] == 0:
                    ready.append((dz, name))
    settle(1e9)

    for dz in range(nz):
        for dx in range(nx):
            if dx or dz:
                arrived(out.at[dev(dx, dz)], osem.at[dx, dz])
    for copy in pending:
        copy.wait_send()


def project(nx, nz, ng, inputs, gain, w, down, qup, vup, spots_and_slots):
    nt = nx * nz
    K2 = inputs.shape[2] // 2
    own = down.shape[0]
    NW = w.shape[0]
    DMA = pltpu.SemaphoreType.DMA
    vmem = pl.BlockSpec(memory_space=pltpu.VMEM)
    hbm = pl.BlockSpec(memory_space=pl.ANY)
    sends = (nt - 1) + (ng - 1) * 6 + 5 * nt + 2 * (nx + nz) + 64 + nt + 160
    rows = nt * 24
    return pl.pallas_call(
        functools.partial(project_kernel, nx, nz, ng, own),
        out_shape=jax.ShapeDtypeStruct((nt, 64, 128), BF16),
        in_specs=[vmem, vmem, hbm, hbm, hbm, hbm, vmem],
        out_specs=vmem,
        scratch_shapes=[
            pltpu.VMEM((nt * 48, K2), BF16),
            pltpu.VMEM((nt * 48, 128), BF16),
            pltpu.VMEM((rows, 128), jnp.int32),
            pltpu.VMEM((2, NW, K2), BF16),
            pltpu.VMEM(vup.shape, BF16),
            pltpu.VMEM((nt * 48, 128), BF16),
            pltpu.VMEM((rows, 256), F32),
            pltpu.VMEM(down.shape, BF16),
            pltpu.VMEM(qup.shape, BF16),
            pltpu.VMEM((own, 64, 128), BF16),
            pltpu.VMEM((ng * 2,) + down.shape[1:], BF16),
            pltpu.VMEM((ng * 2 * 64, 256), BF16),
            pltpu.VMEM((ng * 2 * 64, 128), BF16),
            pltpu.VMEM((ng, 2) + down.shape[1:], BF16),
            pltpu.VMEM((ng, 2, 64, 256), BF16),
            pltpu.VMEM((ng, 2, 64, 128), BF16),
            pltpu.VMEM((ng, 16, 128), jnp.int32),
            pltpu.VMEM((16, 128), jnp.int32),
            pltpu.SMEM((ng, 16, 128), jnp.int32),
            pltpu.VMEM((rows, 128), F32),
            pltpu.VMEM((nx, nz * 24, 128), BF16),
            pltpu.VMEM((nx, nz * 24, 128), BF16),
            pltpu.VMEM((nz, 32, 128), BF16),
            pltpu.VMEM((nz, 32, 128), BF16),
            pltpu.VMEM((nz, 32, 128), BF16),
            pltpu.VMEM((nx, nz, 32, 128), BF16),
            pltpu.VMEM((rows, 128), F32),
            pltpu.VMEM((rows, 128), F32),
            pltpu.VMEM((rows, 256), F32),
            pltpu.VMEM((rows, 128), F32),
            pltpu.VMEM((nz, 2, NW, nx * 48), F32),
            pltpu.VMEM((nz, nx, 64, 128), BF16),
            DMA((sends,)),
            DMA((2, nx, nz, 2)),
            DMA((nt,)),
            DMA((1,)),
            DMA((ng, 5)),
            DMA((ng,)),
            DMA((nx,)),
            DMA((nz,)),
            DMA((nz,)),
            DMA((nx,)),
            DMA((nx, nz)),
            DMA((9,)),
        ],
        compiler_params=pltpu.CompilerParams(
            collective_id=0, has_side_effects=True, vmem_limit_bytes=56 * MIB
        ),
        name="project",
    )(inputs, gain, w, down, qup, vup, spots_and_slots)


def attend_kernel(all_lengths, got, keys, values, out, scr, res, cos, sin):
    rows_here, window, _ = keys.shape
    first_row = lax.axis_index("tensor") * rows_here
    lengths = [all_lengths[first_row + r] for r in range(rows_here)]

    @pl.when(pl.program_id(0) == 0)
    def _():
        sublane = lax.broadcasted_iota(jnp.int32, (8, 128), 0)
        column = lax.broadcasted_iota(jnp.int32, (8, 128), 1)
        ladder = lax.rem(column, 64).astype(F32) * (2.0 / HEAD_DIM)
        inverse = jnp.power(F32(rope_base), -ladder)
        position = jnp.zeros((8, 128), jnp.int32)
        for r in range(rows_here):
            position = jnp.where(sublane == r, lengths[r], position)
        for k in range(3):
            angles = (position + k).astype(F32) * inverse
            cos[8 * k : 8 * k + 8, :] = jnp.cos(angles)
            sine = jnp.sin(angles)
            sin[8 * k : 8 * k + 8, :] = jnp.where(column < 64, -sine, sine)

    factor = HEAD_DIM ** (-0.5)
    dims = (((1,), (1,)), ((), ()))
    lane = lax.broadcasted_iota(jnp.int32, (8, 128), 1) // 32

    def turned(v, c, n):
        return v * c + pltpu.roll(v, 64, 1) * n

    for b in range(8):
        block = got[b].astype(F32)
        for hh in range(2):
            scr[b, hh * 24 : hh * 24 + 24, :] = turned(block[hh * 24 : hh * 24 + 24], cos[...], sin[...])
        scr[b, 48:64, :] = block[48:64]

    def gathered(head, row, offset):
        total = jnp.zeros((8, 128), F32)
        for b in range(4):
            moved = pltpu.roll(scr[4 * head + b, row : row + 8, :], (32 * b - offset) % 128, 1)
            total = jnp.where(lane == b, moved, total)
        return total

    pad = jnp.zeros((8, 128), F32)
    fresh_keys = []
    fresh_values = []
    for e in range(2):
        new = [gathered(e, 48, 0), gathered(e, 48, 64), gathered(e, 56, 0)]
        new = turned(jnp.concatenate(new, axis=0), cos[...], sin[...])
        fresh_keys.append(jnp.concatenate([new, pad], axis=0))
        new = [gathered(e, 48, 32), gathered(e, 48, 96), gathered(e, 56, 32), pad]
        fresh_values.append(jnp.concatenate(new, axis=0))
    fresh_keys = jnp.concatenate(fresh_keys, axis=-1).astype(BF16)
    fresh_values = jnp.concatenate(fresh_values, axis=-1).astype(BF16)

    blank = jnp.zeros((32, 128), F32)
    column = lax.broadcasted_iota(jnp.int32, (64, window), 1)
    queries = []
    past = []
    for r in range(rows_here):
        q = [
            jnp.concatenate([scr[4 * e + b, pl.ds(r, 8, stride=8), :] for b in range(4)], axis=0)
            for e in range(2)
        ]
        q = jnp.concatenate(
            [jnp.concatenate([q[0], blank], axis=-1), jnp.concatenate([blank, q[1]], axis=-1)], axis=0
        ).astype(BF16)
        queries.append(q)
        score = lax.dot_general(q, keys[r], dims, preferred_element_type=F32) * factor
        past.append(jnp.where(column < lengths[r], score, -jnp.inf))
    queries = jnp.concatenate(queries, axis=0)
    past = jnp.concatenate(past, axis=0)
    fresh = lax.dot_general(queries, fresh_keys, dims, preferred_element_type=F32) * factor
    at = lax.broadcasted_iota(jnp.int32, fresh.shape, 0)
    fresh_at = lax.broadcasted_iota(jnp.int32, fresh.shape, 1)
    order = at % 8
    step = jnp.where(order >= 3, order - 3, order)
    own_row = at // 64 == fresh_at % 8
    fresh_live = jnp.logical_and(own_row, jnp.logical_and(fresh_at // 8 <= step, fresh_at < 24))
    fresh = jnp.where(fresh_live, fresh, -jnp.inf)
    highest = jnp.maximum(
        jnp.max(past, axis=-1, keepdims=True), jnp.max(fresh, axis=-1, keepdims=True)
    )
    past = jnp.exp(past - highest)
    fresh = jnp.exp(fresh - highest)
    total = jnp.sum(past, axis=-1, keepdims=True) + jnp.sum(fresh, axis=-1, keepdims=True)
    past = (past / total).astype(BF16)
    fresh = (fresh / total).astype(BF16)
    context = jnp.dot(fresh, fresh_values, preferred_element_type=F32)
    for r in range(rows_here):
        rows = slice(r * 64, (r + 1) * 64)
        part = context[rows] + jnp.dot(past[rows], values[r], preferred_element_type=F32)
        for e in range(2):
            for b in range(4):
                res[4 * e + b, r * 8 : r * 8 + 8, :] = part[
                    32 * e + b * 8 : 32 * e + b * 8 + 8, 128 * e : 128 * e + 128
                ]
    for b in range(8):
        for hh in range(2):
            for k in range(3):
                spot = slice((2 * b + hh) * 128, (2 * b + hh) * 128 + 128)
                out[k, :, spot] = res[b, pl.ds(hh * 3 + k, 8, stride=8), :].astype(BF16)


def attend(all_lengths, got, hist):
    rows, window, width = hist.shape
    steps = 3
    pairs = got.shape[0] // 8
    return pl.pallas_call(
        attend_kernel,
        out_shape=jax.ShapeDtypeStruct((steps, rows, HEADS * HEAD_DIM), BF16),
        grid=(pairs,),
        in_specs=[
            pl.BlockSpec(memory_space=pltpu.SMEM),
            pl.BlockSpec((8, 64, 128), lambda h: (h, 0, 0)),
            pl.BlockSpec((rows, window, 2 * HEAD_DIM), lambda h: (0, 0, h)),
            pl.BlockSpec((rows, window, 2 * HEAD_DIM), lambda h: (0, 0, KV_HEADS // 2 + h)),
        ],
        out_specs=pl.BlockSpec((steps, rows, 2 * HEADS // KV_HEADS * HEAD_DIM), lambda h: (0, 0, h)),
        scratch_shapes=[
            pltpu.VMEM((8, 64, 128), F32),
            pltpu.VMEM((8, 64, 128), F32),
            pltpu.VMEM((steps * rows, 128), F32),
            pltpu.VMEM((steps * rows, 128), F32),
        ],
        compiler_params=pltpu.CompilerParams(vmem_limit_bytes=56 * MIB),
        name="attend",
    )(all_lengths, got, hist, hist)


def routing(adapter_slot, row_adapter, store, groups, home):
    slots = adapter_slot.shape[0]
    catalog = jnp.arange(slots, dtype=jnp.int32)
    by_adapter = row_adapter[:, None] == catalog[None, :]
    slot_of_row = jnp.sum(jnp.where(by_adapter, adapter_slot[None, :], 0), axis=1)
    by_slot = slot_of_row[:, None] == catalog[None, :]
    source = slot_of_row // store
    offset = slot_of_row % store
    wanted = jnp.any(by_slot, axis=0).reshape(groups, store)
    foreign = jnp.logical_and(wanted, jnp.arange(groups, dtype=jnp.int32)[:, None] != home)
    marked = foreign.astype(jnp.int32)
    ranking = jnp.cumsum(marked, axis=1) - marked
    chosen = jnp.logical_and(
        foreign[:, :, None],
        ranking[:, :, None] == jnp.arange(PAIR_MOST, dtype=jnp.int32)[None, None, :],
    )
    request = jnp.sum(
        jnp.where(chosen, jnp.arange(store, dtype=jnp.int32)[None, :, None], 0), axis=1
    )
    row_rank = jnp.sum(jnp.where(by_slot, ranking.reshape(-1)[None, :], 0), axis=1)
    table_row = jnp.where(source == home, offset, store + source * PAIR_MOST + row_rank)
    return request, table_row


def projected(
    inputs, norm_gain, united_weight, adapter_down, query_up, value_up, adapter_slot, row_adapter
):
    steps, rows_here, width = inputs.shape
    nt = lax.axis_size("tensor")
    ng = lax.axis_size("group")
    nx = NX
    nz = nt // nx
    g = lax.axis_index("group")
    request, table_row = routing(adapter_slot, row_adapter, adapter_down.shape[0], ng, g)
    asked = jnp.pad(request.reshape(-1), (0, 16 - ng * PAIR_MOST))
    spots_and_slots = jnp.concatenate([table_row, asked])
    return project(
        nx, nz, ng, inputs, norm_gain, united_weight.T, adapter_down, query_up,
        value_up.transpose(0, 2, 1), spots_and_slots[:, None],
    )


def local(
    inputs, norm_gain, united_weight, adapter_down, query_up, value_up, history,
    adapter_slot, row_adapter, cache_length,
):
    got = projected(
        inputs, norm_gain, united_weight, adapter_down, query_up, value_up, adapter_slot, row_adapter
    )
    return attend(cache_length, got, history)


def solution(mesh):
    in_specs = (
        P(None, ("group", "tensor"), None),
        P(),
        P(None, "tensor"),
        P("group", "tensor", None),
        P("group", None, "tensor"),
        P("group", None, "tensor"),
        P(("group", "tensor"), None, None),
        P(),
        P("group"),
        P("group"),
    )
    out_specs = P(None, ("group", "tensor"), None)
    return jax.shard_map(local, mesh=mesh, in_specs=in_specs, out_specs=out_specs, check_vma=False)
```

```python
import functools
import heapq
import math

import jax
import jax.numpy as jnp
from jax import lax
from jax.experimental import pallas as pl
from jax.experimental.pallas import tpu as pltpu
from jax.sharding import PartitionSpec as P

HEADS = 64
KV_HEADS = 8
HEAD_DIM = 128
PAIR_MOST = 2
NX = 4

adapter_scale = 0.5
rope_base = 500000.0
norm_eps = 1e-05
MIB = 1024 * 1024
F32 = jnp.float32
BF16 = jnp.bfloat16
MESH = pl.DeviceIdType.MESH


CHORES = (3.0, 14.0, 28.0, 40.0, 50.0, 58.0, 66.0)
BUSY = {"x": 4.0, "z": 8.0}
RATE = 39e3
LOOK = 6.0
RANKED = False


def ring_order(nx, nz, la, lb):
    sizes = {"A": la * 96 / RATE, "B": lb * 96 / RATE}
    span = {"x": nx, "z": nz}
    links = [("x", 1), ("x", -1), ("z", 1), ("z", -1)]
    free = {key: BUSY[key[0]] for key in links}
    waiting = {key: [] for key in links}
    asleep = {key: True for key in links}
    heap = []
    halves = {}
    out = []
    count = [0]

    def push(when, what):
        count[0] += 1
        heapq.heappush(heap, (when, count[0], what))

    def send(now, name, dx, dz, half, axis, step, rank):
        key = (axis, step)
        count[0] += 1
        heapq.heappush(waiting[key], (rank, count[0], name, dx % nx, dz % nz, half))
        if asleep[key]:
            asleep[key] = False
            push(max(now, free[key] - LOOK), ("pick", key))

    def rank_of(name, axis, hop):
        if name == "B" and axis == "z":
            return 0
        if name == "A" and axis == "x":
            return 0
        return 5 - hop if RANKED else 1

    def launch(now, name, dx, dz, axis):
        if span[axis] > 2:
            for step in (1, -1):
                send(now, name, dx, dz, None, axis, step, rank_of(name, axis, 0))
        elif span[axis] == 2:
            send(now, name, dx, dz, 0, axis, 1, rank_of(name, axis, 0))
            send(now, name, dx, dz, 1, axis, -1, rank_of(name, axis, 0))

    launch(0.0, "A", 0, 0, "x")
    launch(0.0, "B", 0, 0, "z")
    launch(0.0, "B", 0, 0, "x")
    launch(0.0, "A", 0, 0, "z")
    while heap:
        now, _, what = heapq.heappop(heap)
        if what[0] == "pick":
            key = what[1]
            if not waiting[key]:
                asleep[key] = True
                continue
            _, _, name, dx, dz, half = heapq.heappop(waiting[key])
            axis, step = key
            free[key] = max(free[key], now) + sizes[name] * (1.0 if half is None else 0.5)
            out.append(("send", key, name, dx, dz, half))
            ndx = (dx - (step if axis == "x" else 0)) % nx
            ndz = (dz - (step if axis == "z" else 0)) % nz
            push(free[key] + 1.5, ("land", name, ndx, ndz, half, axis, step))
            push(max(now, free[key] - LOOK), ("pick", key))
            continue
        _, name, dx, dz, half, axis, step = what
        tie = (name, dx, dz)
        seen = halves.get(tie, 0)
        halves[tie] = seen + 1
        last = half is None or seen == 1
        out.append(("wait", now, name, dx, dz, half if half is None else (half, last)))
        size = span[axis]
        far = (-step * (dx if axis == "x" else dz)) % size
        if half is None:
            if far + 1 < size // 2:
                send(now, name, dx, dz, None, axis, step, rank_of(name, axis, far))
            elif far + 1 == size // 2:
                send(now, name, dx, dz, 0 if step > 0 else 1, axis, step, rank_of(name, axis, far))
        if last:
            if name == "A" and axis == "x":
                launch(now, name, dx, dz, "z")
            if name == "B" and axis == "z":
                launch(now, name, dx, dz, "x")
    return out


def project_kernel(
    nx, nz, ng, own,
    inputs, gain, w, down, qup, vup, spots_and_slots,
    out,
    X, xl, tr, wv, vraw, lbuf, xs, down_o, q_o, v_o, down_f, q_f, v_f, sd, sq, sv, rbuf, rsend, rs,
    part, pbuf, S, half_sum, sbuf, lrz, lrall, LRq, LRv, Dq, Dv, plain, ob,
    ssem, gsem, lsem, dsem, fsem, qsem, p1, p2, p3, p4, osem, wsem,
):
    nt = nx * nz
    K2 = X.shape[1]
    NW = w.shape[0]
    rank = 64
    tiles = K2 // 128
    ta = max((tiles * 12) // 32, 2)
    LA = ta * 128
    LB = K2 - LA
    spans = {
        "A": ((0, (ta // 2) * 128), ((ta // 2) * 128, LA - (ta // 2) * 128)),
        "B": ((LA, ((tiles - ta) // 2) * 128), (LA + ((tiles - ta) // 2) * 128, LB - ((tiles - ta) // 2) * 128)),
    }
    whole = {"A": (0, LA), "B": (LA, LB)}
    which = {"A": 0, "B": 1}

    g = lax.axis_index("group")
    t = lax.axis_index("tensor")
    z = t // nx
    x = t % nx

    def dev(dx, dz):
        return lax.rem(z + (dz % nz), nz) * nx + lax.rem(x + (dx % nx), nx)

    pending = []
    counter = [0]

    def remote(src, dst, rsem, group, tensor):
        sem = ssem.at[counter[0]]
        counter[0] += 1
        copy = pltpu.make_async_remote_copy(
            src_ref=src, dst_ref=dst, send_sem=sem, recv_sem=rsem,
            device_id=(group, tensor), device_id_type=MESH,
        )
        copy.start()
        pending.append(copy)

    def arrived(ref, sem):
        pltpu.make_async_copy(ref, ref, sem).wait()

    barrier = pltpu.get_barrier_semaphore()

    def greet(k, carry):
        pl.semaphore_signal(barrier, inc=1, device_id=(g, lax.rem(t + k, nt)), device_id_type=MESH)
        return carry

    lax.fori_loop(1, nt, greet, 0)

    def greet_group(k, carry):
        pl.semaphore_signal(barrier, inc=1, device_id=(lax.rem(g + k, ng), t), device_id_type=MESH)
        return carry

    lax.fori_loop(1, ng, greet_group, 0)

    mine = pl.multiple_of(t * 48, 16)
    loads = [
        pltpu.make_async_copy(down, down_o, wsem.at[1]),
        pltpu.make_async_copy(qup, q_o, wsem.at[2]),
        pltpu.make_async_copy(vup, vraw, wsem.at[3]),
        pltpu.make_async_copy(w.at[:, pl.ds(0, K2)], wv.at[0], wsem.at[4]),
        pltpu.make_async_copy(w.at[:, pl.ds(K2, K2)], wv.at[1], wsem.at[5]),
    ]
    for load in loads:
        load.start()

    values = inputs[...].astype(F32)
    mean_square = jnp.mean(values * values, axis=-1, keepdims=True)
    normed = values * lax.rsqrt(mean_square + norm_eps) * gain[...].astype(F32).reshape(1, 1, 2 * K2)
    for step in range(3):
        halves = jnp.concatenate([normed[step, :, :K2], normed[step, :, K2:]], axis=0)
        X[pl.ds(pl.multiple_of(mine + step * 16, 16), 16), :] = halves.astype(BF16)
    for p in range(nt):
        pieces = [normed[step, :, p * 256 + h * 128 : p * 256 + h * 128 + 128] for h in range(2) for step in range(3)]
        xl[p * 48 : p * 48 + 48, :] = jnp.concatenate(pieces, axis=0).astype(BF16)
    lbuf[pl.ds(mine, 48), :] = xl[pl.ds(mine, 48), :]
    rsend[...] = jnp.broadcast_to(spots_and_slots[nt * 8 : nt * 8 + 16, :], (16, 128))
    spots = jnp.broadcast_to(spots_and_slots[0 : nt * 8, :], (nt * 8, 128)).reshape(nt, 1, 8, 128)
    tr[...] = jnp.broadcast_to(spots, (nt, 3, 8, 128)).reshape(nt * 24, 128)

    pl.semaphore_wait(barrier, nt - 1 + ng - 1)

    def piece(dx, dz, lo, n):
        rows = pl.multiple_of(dev(dx, dz) * 48, 16)
        return X.at[pl.ds(rows, 48), pl.ds(lo, n)]

    def forward(name, dx, dz, half, axis, step):
        lo, n = whole[name] if half is None else spans[name][half]
        ref = piece(dx, dz, lo, n)
        if axis == "x":
            there = dev(step, 0)
            ndx, ndz = (dx - step) % nx, dz % nz
        else:
            there = dev(0, step)
            ndx, ndz = dx % nx, (dz - step) % nz
        remote(ref, ref, gsem.at[which[name], ndx, ndz, 0 if half is None else half], g, there)

    def expect(name, dx, dz, half):
        lo, n = whole[name] if half is None else spans[name][half]
        arrived(piece(dx, dz, lo, n), gsem.at[which[name], dx % nx, dz % nz, 0 if half is None else half])

    for k in range(1, nt):
        peer = lax.rem(t + k, nt)
        remote(
            xl.at[pl.ds(pl.multiple_of(peer * 48, 16), 48), :],
            lbuf.at[pl.ds(mine, 48), :], lsem.at[nt - k], g, peer,
        )
    for k in range(1, ng):
        peer = lax.rem(g + k, ng)
        remote(rsend, rbuf.at[g], qsem.at[ng - k], peer, t)

    def lend():
        for load in loads[0:3]:
            load.wait()
        def turn(e, carry):
            column = vraw[e].astype(F32).T
            left = jnp.zeros((rank, 32), F32)
            right = jnp.zeros((rank, 64), F32)
            v_o[e] = jnp.concatenate([left, column, right], axis=-1).astype(BF16)
            return carry

        lax.fori_loop(0, own, turn, 0)
        down_f[pl.ds(g * 2, 2)] = jnp.zeros((2,) + down_f.shape[1:], BF16)
        own_spot = pl.ds(pl.multiple_of(g * 2 * rank, 16), 2 * rank)
        q_f[own_spot, :] = jnp.zeros((2 * rank, q_f.shape[1]), BF16)
        v_f[own_spot, :] = jnp.zeros((2 * rank, v_f.shape[1]), BF16)
        for k in range(1, ng):
            peer = lax.rem(g + k, ng)
            arrived(rbuf.at[peer], qsem.at[k])
            down_copy = pltpu.make_async_copy(rbuf.at[peer], rs.at[k], wsem.at[7])
            down_copy.start()
            down_copy.wait()
            for j in range(PAIR_MOST):
                slot = rs[k, PAIR_MOST * g + j, 0]
                sd[k, j] = down_o[slot]
                sq[k, j] = q_o[slot]
                sv[k, j] = v_o[slot]
            remote(sd.at[k], down_f.at[pl.ds(g * 2, 2)], fsem.at[ng - k, 0], peer, t)
            for j in range(PAIR_MOST):
                spot = pl.ds(pl.multiple_of((g * 2 + j) * rank, 16), rank)
                remote(sq.at[k, j], q_f.at[spot, :], fsem.at[ng - k, 1 + j], peer, t)
                remote(sv.at[k, j], v_f.at[spot, :], fsem.at[ng - k, 3 + j], peer, t)

    def shrink(table, first):
        def body(e, carry):
            chosen = tr[...] == e + first
            pick = jnp.concatenate([chosen, chosen], axis=-1)
            rows = jnp.where(pick, xs[...], 0.0).astype(BF16)
            part[...] += jnp.dot(rows, table[e], preferred_element_type=F32)
            return carry
        return body

    def shrink_own():
        for k in range(1, nt):
            arrived(lbuf.at[pl.ds(pl.multiple_of(lax.rem(t + k, nt) * 48, 16), 48), :], lsem.at[k])
        both = lbuf[...].astype(F32).reshape(nt, 2, 24, 128)
        xs[...] = jnp.concatenate([both[:, 0], both[:, 1]], axis=-1).reshape(nt * 24, 256)
        part[...] = jnp.zeros(part.shape, F32)
        lax.fori_loop(0, own, shrink(down_o, 0), 0)

    def shrink_far():
        for k in range(1, ng):
            peer = lax.rem(g + k, ng)
            arrived(down_f.at[pl.ds(peer * 2, 2)], fsem.at[k, 0])
        lax.fori_loop(0, ng * PAIR_MOST, shrink(down_f, own), 0)
        whole_part = part[...].reshape(nz, nx, 24, 128)
        for xx in range(nx):
            S[xx] = whole_part[:, xx].reshape(nz * 24, 128).astype(BF16)
        for k in range(1, nx):
            peer = lax.rem(x + k, nx)
            remote(S.at[peer], pbuf.at[x], p1.at[nx - k], g, z * nx + peer)

    def sum_x():
        pbuf[pl.ds(x, 1)] = S[pl.ds(x, 1)]
        for k in range(1, nx):
            arrived(pbuf.at[lax.rem(x + k, nx)], p1.at[k])
        total = pbuf[0].astype(F32)
        for xx in range(1, nx):
            total = total + pbuf[xx].astype(F32)
        blank = jnp.zeros((8, 128), F32)
        for zz in range(nz):
            half_sum[zz] = jnp.concatenate([total[zz * 24 : zz * 24 + 24], blank], axis=0).astype(BF16)
        for k in range(1, nz):
            peer = lax.rem(z + k, nz)
            remote(half_sum.at[peer], sbuf.at[z], p2.at[nz - k], g, peer * nx + x)

    def sum_z():
        sbuf[pl.ds(z, 1)] = half_sum[pl.ds(z, 1)]
        for k in range(1, nz):
            arrived(sbuf.at[lax.rem(z + k, nz)], p2.at[k])
        low = sbuf[0].astype(F32)
        for zz in range(1, nz):
            low = low + sbuf[zz].astype(F32)
        lrz[pl.ds(z, 1)] = low.astype(BF16)[None]
        for k in range(1, nz):
            peer = lax.rem(z + k, nz)
            remote(lrz.at[z], lrz.at[z], p3.at[nz - k], g, peer * nx + x)

    def spread_x():
        for k in range(1, nz):
            arrived(lrz.at[lax.rem(z + k, nz)], p3.at[k])
        lrall[pl.ds(x, 1)] = lrz[...][None]
        for k in range(1, nx):
            peer = lax.rem(x + k, nx)
            remote(lrz, lrall.at[x], p4.at[nx - k], g, z * nx + peer)

    def expand():
        for k in range(1, nx):
            arrived(lrall.at[lax.rem(x + k, nx)], p4.at[k])
        for k in range(1, ng):
            peer = lax.rem(g + k, ng)
            for j in range(PAIR_MOST):
                spot = pl.ds(pl.multiple_of((peer * 2 + j) * rank, 16), rank)
                arrived(q_f.at[spot, :], fsem.at[k, 1 + j])
                arrived(v_f.at[spot, :], fsem.at[k, 3 + j])

        for zz in range(nz):
            for xx in range(nx):
                low24 = lrall[xx, zz].astype(F32)[:24]
                spot = pl.ds((zz * nx + xx) * 24, 24)
                LRq[spot, :] = jnp.concatenate([low24[:, :64], low24[:, :64]], axis=-1)
                LRv[spot, :] = jnp.concatenate([low24[:, 64:], low24[:, 64:]], axis=-1)
        Dq[...] = jnp.zeros(Dq.shape, F32)
        Dv[...] = jnp.zeros(Dv.shape, F32)

        def grow(q_table, v_table, first):
            def body(i, carry):
                lane = lax.broadcasted_iota(jnp.int32, (nt * 24, 128), 1) // 64
                hit0 = tr[...] == lane + (i * 4 + first)
                hit1 = tr[...] == lane + (i * 4 + 2 + first)
                spread_q = jnp.concatenate([jnp.where(hit0, LRq[...], 0.0), jnp.where(hit1, LRq[...], 0.0)], axis=-1)
                spread_v = jnp.concatenate([jnp.where(hit0, LRv[...], 0.0), jnp.where(hit1, LRv[...], 0.0)], axis=-1)
                Dq[...] += jnp.dot(spread_q.astype(BF16), q_table(i), preferred_element_type=F32)
                Dv[...] += jnp.dot(spread_v.astype(BF16), v_table(i), preferred_element_type=F32)
                return carry
            return body

        def own_table(ref):
            return lambda i: ref[pl.ds(i * 4, 4)].reshape(4 * rank, ref.shape[2])

        def far_table(ref):
            return lambda i: ref[pl.ds(pl.multiple_of(i * 4 * rank, 4 * rank), 4 * rank), :]

        lax.fori_loop(0, own // 4, grow(own_table(q_o), own_table(v_o), 0), 0)
        lax.fori_loop(0, ng * PAIR_MOST // 4, grow(far_table(q_f), far_table(v_f), own), 0)

    kt = 128 * math.gcd(ta, tiles, 4)
    seen = {dz: [] for dz in range(nz)}

    def multiply(dz, name):
        rows = pl.ds(pl.multiple_of(lax.rem(z + dz % nz, nz) * (nx * 48), 16), nx * 48)
        lo, n = whole[name]

        def body(k, carry):
            cols = pl.ds(pl.multiple_of(lo + k * kt, kt), kt)
            for h in range(2):
                plain[dz, h] += lax.dot_general(
                    wv[h, :, cols], X[rows, cols], (((1,), (1,)), ((), ())), preferred_element_type=F32
                )
            return carry

        if name not in seen[dz] and not seen[dz]:
            plain[dz] = jnp.zeros(plain.shape[1:], F32)
        seen[dz].append(name)
        lax.fori_loop(0, n // kt, body, 0)

    def base_of(dz):
        first = plain[dz, 0].T.reshape(nx * 3, 2, 8, NW)[:, 0]
        second = plain[dz, 1].T.reshape(nx * 3, 2, 8, NW)[:, 1]
        return (first + second).reshape(nx * 24, NW)

    def finish(dz):
        base = base_of(dz % nz)
        zz = lax.rem(z + dz % nz, nz)
        rows = pl.ds(pl.multiple_of(zz * (nx * 24), 8), nx * 24)
        query = base[:, :256] + adapter_scale * Dq[rows, :]
        keyval = base[:, 256:320] + adapter_scale * Dv[rows, :][:, :64]
        for xx in range(nx):
            q = query[xx * 24 : xx * 24 + 24]
            kv = keyval[xx * 24 : xx * 24 + 24]
            block = jnp.concatenate(
                [
                    q[:, :128], q[:, 128:],
                    jnp.concatenate([kv[0:8], kv[8:16]], axis=-1),
                    jnp.concatenate([kv[16:24], jnp.zeros((8, 64), F32)], axis=-1),
                ],
                axis=0,
            )
            ob[dz % nz, xx] = block.astype(BF16)
        for dx in range(nx):
            xx = lax.rem(x + dx, nx)
            if dx == 0 and dz % nz == 0:
                keep = pltpu.make_async_copy(ob.at[0, xx], out.at[t], wsem.at[8])
                keep.start()
                keep.wait()
            else:
                remote(ob.at[dz % nz, xx], out.at[t], osem.at[(-dx) % nx, (-dz) % nz], g, zz * nx + xx)

    chores = [
        (CHORES[0], lend), (CHORES[1], shrink_own), (CHORES[2], shrink_far), (CHORES[3], sum_x),
        (CHORES[4], sum_z), (CHORES[5], spread_x), (CHORES[6], expand),
    ]
    loaded = []
    ready = []
    based = []
    missing = {(dz, name): nx - (dz == 0) for dz in range(nz) for name in "AB"}

    def settle(now):
        while chores and chores[0][0] <= now:
            chores.pop(0)[1]()
        while ready:
            if not loaded:
                for load in loads[3:5]:
                    load.wait()
                loaded.append(1)
            dz, name = ready.pop(0)
            multiply(dz, name)
            if len(seen[dz]) == 2:
                based.append(dz)
        while based and not chores:
            finish(based.pop(0))

    for kind, when, name, dx, dz, half in ring_order(nx, nz, LA, LB):
        if kind == "send":
            axis, step = when
            forward(name, dx, dz, half, axis, step)
        else:
            settle(when)
            piece_half, last = (None, True) if half is None else half
            expect(name, dx, dz, piece_half)
            if last:
                missing[dz, name] -= 1
                if missing[dz, name] == 0:
                    ready.append((dz, name))
    settle(1e9)

    for dz in range(nz):
        for dx in range(nx):
            if dx or dz:
                arrived(out.at[dev(dx, dz)], osem.at[dx, dz])
    for copy in pending:
        copy.wait_send()


def project(nx, nz, ng, inputs, gain, w, down, qup, vup, spots_and_slots):
    nt = nx * nz
    K2 = inputs.shape[2] // 2
    own = down.shape[0]
    NW = w.shape[0]
    DMA = pltpu.SemaphoreType.DMA
    vmem = pl.BlockSpec(memory_space=pltpu.VMEM)
    hbm = pl.BlockSpec(memory_space=pl.ANY)
    sends = (nt - 1) + (ng - 1) * 6 + 5 * nt + 2 * (nx + nz) + 64 + nt + 160
    rows = nt * 24
    return pl.pallas_call(
        functools.partial(project_kernel, nx, nz, ng, own),
        out_shape=jax.ShapeDtypeStruct((nt, 64, 128), BF16),
        in_specs=[vmem, vmem, hbm, hbm, hbm, hbm, vmem],
        out_specs=vmem,
        scratch_shapes=[
            pltpu.VMEM((nt * 48, K2), BF16),
            pltpu.VMEM((nt * 48, 128), BF16),
            pltpu.VMEM((rows, 128), jnp.int32),
            pltpu.VMEM((2, NW, K2), BF16),
            pltpu.VMEM(vup.shape, BF16),
            pltpu.VMEM((nt * 48, 128), BF16),
            pltpu.VMEM((rows, 256), F32),
            pltpu.VMEM(down.shape, BF16),
            pltpu.VMEM(qup.shape, BF16),
            pltpu.VMEM((own, 64, 128), BF16),
            pltpu.VMEM((ng * 2,) + down.shape[1:], BF16),
            pltpu.VMEM((ng * 2 * 64, 256), BF16),
            pltpu.VMEM((ng * 2 * 64, 128), BF16),
            pltpu.VMEM((ng, 2) + down.shape[1:], BF16),
            pltpu.VMEM((ng, 2, 64, 256), BF16),
            pltpu.VMEM((ng, 2, 64, 128), BF16),
            pltpu.VMEM((ng, 16, 128), jnp.int32),
            pltpu.VMEM((16, 128), jnp.int32),
            pltpu.SMEM((ng, 16, 128), jnp.int32),
            pltpu.VMEM((rows, 128), F32),
            pltpu.VMEM((nx, nz * 24, 128), BF16),
            pltpu.VMEM((nx, nz * 24, 128), BF16),
            pltpu.VMEM((nz, 32, 128), BF16),
            pltpu.VMEM((nz, 32, 128), BF16),
            pltpu.VMEM((nz, 32, 128), BF16),
            pltpu.VMEM((nx, nz, 32, 128), BF16),
            pltpu.VMEM((rows, 128), F32),
            pltpu.VMEM((rows, 128), F32),
            pltpu.VMEM((rows, 256), F32),
            pltpu.VMEM((rows, 128), F32),
            pltpu.VMEM((nz, 2, NW, nx * 48), F32),
            pltpu.VMEM((nz, nx, 64, 128), BF16),
            DMA((sends,)),
            DMA((2, nx, nz, 2)),
            DMA((nt,)),
            DMA((1,)),
            DMA((ng, 5)),
            DMA((ng,)),
            DMA((nx,)),
            DMA((nz,)),
            DMA((nz,)),
            DMA((nx,)),
            DMA((nx, nz)),
            DMA((9,)),
        ],
        compiler_params=pltpu.CompilerParams(
            collective_id=0, has_side_effects=True, vmem_limit_bytes=56 * MIB
        ),
        name="project",
    )(inputs, gain, w, down, qup, vup, spots_and_slots)


def attend_kernel(all_lengths, got, keys, values, out, scr, res, cos, sin):
    rows_here, window, _ = keys.shape
    first_row = lax.axis_index("tensor") * rows_here
    lengths = [all_lengths[first_row + r] for r in range(rows_here)]

    @pl.when(pl.program_id(0) == 0)
    def _():
        sublane = lax.broadcasted_iota(jnp.int32, (8, 128), 0)
        column = lax.broadcasted_iota(jnp.int32, (8, 128), 1)
        ladder = lax.rem(column, 64).astype(F32) * (2.0 / HEAD_DIM)
        inverse = jnp.power(F32(rope_base), -ladder)
        position = jnp.zeros((8, 128), jnp.int32)
        for r in range(rows_here):
            position = jnp.where(sublane == r, lengths[r], position)
        for k in range(3):
            angles = (position + k).astype(F32) * inverse
            cos[8 * k : 8 * k + 8, :] = jnp.cos(angles)
            sine = jnp.sin(angles)
            sin[8 * k : 8 * k + 8, :] = jnp.where(column < 64, -sine, sine)

    factor = HEAD_DIM ** (-0.5)
    dims = (((1,), (1,)), ((), ()))
    lane = lax.broadcasted_iota(jnp.int32, (8, 128), 1) // 32

    def turned(v, c, n):
        return v * c + pltpu.roll(v, 64, 1) * n

    for b in range(8):
        block = got[b].astype(F32)
        for hh in range(2):
            scr[b, hh * 24 : hh * 24 + 24, :] = turned(block[hh * 24 : hh * 24 + 24], cos[...], sin[...])
        scr[b, 48:64, :] = block[48:64]

    def gathered(head, row, offset):
        total = jnp.zeros((8, 128), F32)
        for b in range(4):
            moved = pltpu.roll(scr[4 * head + b, row : row + 8, :], (32 * b - offset) % 128, 1)
            total = jnp.where(lane == b, moved, total)
        return total

    pad = jnp.zeros((8, 128), F32)
    fresh_keys = []
    fresh_values = []
    for e in range(2):
        new = [gathered(e, 48, 0), gathered(e, 48, 64), gathered(e, 56, 0)]
        new = turned(jnp.concatenate(new, axis=0), cos[...], sin[...])
        fresh_keys.append(jnp.concatenate([new, pad], axis=0))
        new = [gathered(e, 48, 32), gathered(e, 48, 96), gathered(e, 56, 32), pad]
        fresh_values.append(jnp.concatenate(new, axis=0))
    fresh_keys = jnp.concatenate(fresh_keys, axis=-1).astype(BF16)
    fresh_values = jnp.concatenate(fresh_values, axis=-1).astype(BF16)

    blank = jnp.zeros((32, 128), F32)
    column = lax.broadcasted_iota(jnp.int32, (64, window), 1)
    queries = []
    past = []
    for r in range(rows_here):
        q = [
            jnp.concatenate([scr[4 * e + b, pl.ds(r, 8, stride=8), :] for b in range(4)], axis=0)
            for e in range(2)
        ]
        q = jnp.concatenate(
            [jnp.concatenate([q[0], blank], axis=-1), jnp.concatenate([blank, q[1]], axis=-1)], axis=0
        ).astype(BF16)
        queries.append(q)
        score = lax.dot_general(q, keys[r], dims, preferred_element_type=F32) * factor
        past.append(jnp.where(column < lengths[r], score, -jnp.inf))
    queries = jnp.concatenate(queries, axis=0)
    past = jnp.concatenate(past, axis=0)
    fresh = lax.dot_general(queries, fresh_keys, dims, preferred_element_type=F32) * factor
    at = lax.broadcasted_iota(jnp.int32, fresh.shape, 0)
    fresh_at = lax.broadcasted_iota(jnp.int32, fresh.shape, 1)
    order = at % 8
    step = jnp.where(order >= 3, order - 3, order)
    own_row = at // 64 == fresh_at % 8
    fresh_live = jnp.logical_and(own_row, jnp.logical_and(fresh_at // 8 <= step, fresh_at < 24))
    fresh = jnp.where(fresh_live, fresh, -jnp.inf)
    highest = jnp.maximum(
        jnp.max(past, axis=-1, keepdims=True), jnp.max(fresh, axis=-1, keepdims=True)
    )
    past = jnp.exp(past - highest)
    fresh = jnp.exp(fresh - highest)
    total = jnp.sum(past, axis=-1, keepdims=True) + jnp.sum(fresh, axis=-1, keepdims=True)
    past = (past / total).astype(BF16)
    fresh = (fresh / total).astype(BF16)
    context = jnp.dot(fresh, fresh_values, preferred_element_type=F32)
    for r in range(rows_here):
        rows = slice(r * 64, (r + 1) * 64)
        part = context[rows] + jnp.dot(past[rows], values[r], preferred_element_type=F32)
        for e in range(2):
            for b in range(4):
                res[4 * e + b, r * 8 : r * 8 + 8, :] = part[
                    32 * e + b * 8 : 32 * e + b * 8 + 8, 128 * e : 128 * e + 128
                ]
    for b in range(8):
        for hh in range(2):
            for k in range(3):
                spot = slice((2 * b + hh) * 128, (2 * b + hh) * 128 + 128)
                out[k, :, spot] = res[b, pl.ds(hh * 3 + k, 8, stride=8), :].astype(BF16)


def attend(all_lengths, got, hist):
    rows, window, width = hist.shape
    steps = 3
    pairs = got.shape[0] // 8
    return pl.pallas_call(
        attend_kernel,
        out_shape=jax.ShapeDtypeStruct((steps, rows, HEADS * HEAD_DIM), BF16),
        grid=(pairs,),
        in_specs=[
            pl.BlockSpec(memory_space=pltpu.SMEM),
            pl.BlockSpec((8, 64, 128), lambda h: (h, 0, 0)),
            pl.BlockSpec((rows, window, 2 * HEAD_DIM), lambda h: (0, 0, h)),
            pl.BlockSpec((rows, window, 2 * HEAD_DIM), lambda h: (0, 0, KV_HEADS // 2 + h)),
        ],
        out_specs=pl.BlockSpec((steps, rows, 2 * HEADS // KV_HEADS * HEAD_DIM), lambda h: (0, 0, h)),
        scratch_shapes=[
            pltpu.VMEM((8, 64, 128), F32),
            pltpu.VMEM((8, 64, 128), F32),
            pltpu.VMEM((steps * rows, 128), F32),
            pltpu.VMEM((steps * rows, 128), F32),
        ],
        compiler_params=pltpu.CompilerParams(vmem_limit_bytes=56 * MIB),
        name="attend",
    )(all_lengths, got, hist, hist)


def routing(adapter_slot, row_adapter, store, groups, home):
    slots = adapter_slot.shape[0]
    catalog = jnp.arange(slots, dtype=jnp.int32)
    by_adapter = row_adapter[:, None] == catalog[None, :]
    slot_of_row = jnp.sum(jnp.where(by_adapter, adapter_slot[None, :], 0), axis=1)
    by_slot = slot_of_row[:, None] == catalog[None, :]
    source = slot_of_row // store
    offset = slot_of_row % store
    wanted = jnp.any(by_slot, axis=0).reshape(groups, store)
    foreign = jnp.logical_and(wanted, jnp.arange(groups, dtype=jnp.int32)[:, None] != home)
    marked = foreign.astype(jnp.int32)
    ranking = jnp.cumsum(marked, axis=1) - marked
    chosen = jnp.logical_and(
        foreign[:, :, None],
        ranking[:, :, None] == jnp.arange(PAIR_MOST, dtype=jnp.int32)[None, None, :],
    )
    request = jnp.sum(
        jnp.where(chosen, jnp.arange(store, dtype=jnp.int32)[None, :, None], 0), axis=1
    )
    row_rank = jnp.sum(jnp.where(by_slot, ranking.reshape(-1)[None, :], 0), axis=1)
    table_row = jnp.where(source == home, offset, store + source * PAIR_MOST + row_rank)
    return request, table_row


def projected(
    inputs, norm_gain, united_weight, adapter_down, query_up, value_up, adapter_slot, row_adapter
):
    steps, rows_here, width = inputs.shape
    nt = lax.axis_size("tensor")
    ng = lax.axis_size("group")
    nx = NX
    nz = nt // nx
    g = lax.axis_index("group")
    request, table_row = routing(adapter_slot, row_adapter, adapter_down.shape[0], ng, g)
    asked = jnp.pad(request.reshape(-1), (0, 16 - ng * PAIR_MOST))
    spots_and_slots = jnp.concatenate([table_row, asked])
    return project(
        nx, nz, ng, inputs, norm_gain, united_weight.T, adapter_down, query_up,
        value_up.transpose(0, 2, 1), spots_and_slots[:, None],
    )


def local(
    inputs, norm_gain, united_weight, adapter_down, query_up, value_up, history,
    adapter_slot, row_adapter, cache_length,
):
    got = projected(
        inputs, norm_gain, united_weight, adapter_down, query_up, value_up, adapter_slot, row_adapter
    )
    return attend(cache_length, got, history)


def solution(mesh):
    in_specs = (
        P(None, ("group", "tensor"), None),
        P(),
        P(None, "tensor"),
        P("group", "tensor", None),
        P("group", None, "tensor"),
        P("group", None, "tensor"),
        P(("group", "tensor"), None, None),
        P(),
        P("group"),
        P("group"),
    )
    out_specs = P(None, ("group", "tensor"), None)
    return jax.shard_map(local, mesh=mesh, in_specs=in_specs, out_specs=out_specs, check_vma=False)
```
